32 devices in a mesh: dom: 8 (over z, x), tp: 4 (over y, core).
Axes of the slice: x: 2, y: 2, z: 4, core: 2. Of those that a mesh axis runs over, the one named last changes fastest.
Arguments:
- state: bfloat16 [2, 8192, 512], P(None, 'dom'), may hold values from -6 to 6
- norm_gain: float32 [2, 2, 512], replicated, may hold values from 0.1 to 1.9
- norm_shift: float32 [2, 2, 512], replicated, may hold values from -3 to 3
- qkv_weight: bfloat16 [512, 3, 512], P(None, None, 'tp'), may hold values from -0.5 to 0.5
- out_weight: bfloat16 [512, 512], P('tp'), may hold values from -0.25 to 0.25
- up_weight: bfloat16 [512, 2048], P(None, 'tp'), may hold values from -0.25 to 0.25
- down_weight: bfloat16 [2048, 512], P('tp'), may hold values from -0.125 to 0.125
- neighbours: int32 [64, 8], P('dom'), may hold values from 0 to 63, as said below
- counts: int32 [64], P('dom'), may hold values from 2 to 8, as said below
Outputs:
- layer_out: bfloat16 [2, 8192, 512], P(None, 'dom', 'tp')
The draws below stay inside these ranges and needn't reach their ends.
Inputs may be any that keep to these rules, and one draw needn't show every extreme that they name: `neighbours`: entry 0 of row b is b itself; the other 7 entries are distinct blocks whose partition (block // 8) lies at most two partitions before or after b's on a closed chain of partitions, block numbers taken modulo 64. `counts`: every partition has a block whose count is 8.
All inputs are finite; a program needn't handle non-finite values.
Results may differ from the reference program's by a relative error of at most 0.017.
Values may be sent and summed in bfloat16 or wider, within the bound.
A program may use at most 64 MiB of HBM per device.

```python
import math
import jax
import jax.numpy as jnp
from jax import lax

D = 512
HEADS = 4
FF = 2048
NODE_BLK = 128
KMAX = 8
S = 2
BLK_DEV = 8
BLOCKS = 64
NODES = 8192
N_TP = 4


def draw_neighbours(key, part):
    window = 5 * BLK_DEV
    row_keys = jax.random.split(key, BLOCKS)

    def one_row(row_key, block_id):
        chosen_slots = jax.random.permutation(row_key, window - 1)[:KMAX - 1]
        within = block_id % BLK_DEV
        self_slot = 2 * BLK_DEV + within
        offsets = chosen_slots + (chosen_slots >= self_slot).astype(jnp.int32)
        others = jnp.mod(block_id - within - 2 * BLK_DEV + offsets, BLOCKS)
        return jnp.concatenate([block_id[None], others]).astype(jnp.int32)
    return jax.vmap(one_row)(row_keys, jnp.arange(BLOCKS, dtype=jnp.int32))


def draw_counts(key, part):
    base_counts = jax.random.randint(key, (BLOCKS,), 2, KMAX + 1)
    full_slot = jax.random.randint(jax.random.fold_in(key, 7), (BLOCKS // BLK_DEV,), 0, BLK_DEV)
    within = jnp.arange(BLOCKS, dtype=jnp.int32) % BLK_DEV
    return jnp.where(within == jnp.repeat(full_slot, BLK_DEV), KMAX, base_counts).astype(jnp.int32)


def shard_levels(rng, extent, cuts, least, largest):
    def one(position, blocks):
        heights = jax.random.uniform(jax.random.fold_in(jax.random.fold_in(rng, 6), position), (blocks,), jnp.float32, least / len(cuts), largest / len(cuts))
        return jnp.repeat(jnp.exp(heights), extent[position] // blocks).reshape((-1,) + (1,) * (len(extent) - position - 1))

    factor_of = one(*cuts[0])
    for cut in cuts[1:]:
        factor_of = factor_of * one(*cut)
    return factor_of


def gaussian(rng, extent, deviation, reach, pieces=(), held_as=jnp.bfloat16):
    entries = jax.random.normal(rng, extent, jnp.float32) * deviation
    if len(pieces) > 0:
        entries = shard_levels(rng, extent, pieces, -0.22, 0.18) * entries
    return jnp.clip(entries, min=-reach, max=reach).astype(held_as)


def setup_inputs(seed: int = 0) -> dict:
    keys = jax.random.split(jax.random.key(seed), 10)
    return {
        "state": gaussian(keys[0], (S, NODES, D), 1.0, 6.0, ((1, 8),)),
        "norm_gain": jnp.clip(1.0 + 0.18 * jax.random.normal(keys[1], (2, S, D), jnp.float32), 0.1, 1.9),
        "norm_shift": gaussian(keys[2], (2, S, D), 0.5, 3.0, (), jnp.float32),
        "qkv_weight": gaussian(keys[3], (D, 3, D), (D // 4) ** -0.5, 0.5, ((2, 4),)),
        "out_weight": gaussian(keys[4], (D, D), D ** -0.5, 0.25, ((0, 4),)),
        "up_weight": gaussian(keys[5], (D, FF), D ** -0.5, 0.25, ((1, 4),)),
        "down_weight": gaussian(keys[6], (FF, D), FF ** -0.5, 0.125, ((0, 4),)),
        "neighbours": draw_neighbours(jax.random.fold_in(keys[9], 71), 0),
        "counts": draw_counts(jax.random.fold_in(keys[9], 71), 0),
    }


def layer_norm(values, gain_row, shift_row):
    row_mean = lax.optimization_barrier(jnp.mean(values, axis=-1, keepdims=True))
    centred = values - row_mean
    spread = lax.optimization_barrier(jnp.mean(centred * centred, axis=-1, keepdims=True))
    return centred * lax.rsqrt(spread + 1e-05) * gain_row + shift_row

def reference(state, norm_gain, norm_shift, qkv_weight, out_weight, up_weight, down_weight, neighbours, counts):
    samples, node_count, feat_width = state.shape
    block_count = node_count // NODE_BLK
    head_size = feat_width // HEADS
    head_cols = feat_width // N_TP
    unit_cols = FF // N_TP
    resid_in = state.astype(jnp.float32)
    normed = layer_norm(resid_in, norm_gain[0][:, None, :], norm_shift[0][:, None, :]).astype(jnp.bfloat16)
    projected = jnp.einsum('snd,dce->snce', normed.astype(jnp.float32), qkv_weight.astype(jnp.float32)).astype(jnp.bfloat16)
    projected = projected.reshape(samples, block_count, NODE_BLK, 3, HEADS, head_size)
    slot_ids = jnp.arange(KMAX * NODE_BLK, dtype=jnp.int32) // NODE_BLK

    def attend(block_idx):
        queries = projected[:, block_idx, :, 0].astype(jnp.float32)
        chosen = projected[:, neighbours[block_idx]]
        chosen = chosen.reshape(samples, KMAX * NODE_BLK, 3, HEADS, head_size).astype(jnp.float32)
        scores = jnp.einsum('sqhe,skhe->shqk', queries, chosen[:, :, 1]) / math.sqrt(head_size)
        live_mask = slot_ids < counts[block_idx]
        masked = jnp.where(live_mask, scores, -1e+30)
        row_top = lax.optimization_barrier(jnp.max(masked, axis=-1, keepdims=True))
        weights = jnp.exp(masked - row_top)
        weights = (weights / lax.optimization_barrier(jnp.sum(weights, axis=-1, keepdims=True))).astype(jnp.bfloat16)
        return jnp.einsum('shqk,skhe->sqhe', weights.astype(jnp.float32), chosen[:, :, 2]).astype(jnp.bfloat16)
    heads_out = lax.map(attend, jnp.arange(block_count, dtype=jnp.int32))
    heads_out = jnp.transpose(heads_out, (1, 0, 2, 3, 4)).reshape(samples * node_count, feat_width)
    attn_sum = jnp.zeros((samples * node_count, feat_width), jnp.float32)
    for tp_rank in range(N_TP):
        col_first = tp_rank * head_cols
        term_part = jnp.dot(heads_out[:, col_first:col_first + head_cols], out_weight[col_first:col_first + head_cols], preferred_element_type=jnp.float32).astype(jnp.bfloat16)
        term_part = lax.optimization_barrier(term_part)
        attn_sum = attn_sum + term_part.astype(jnp.float32)
    residual = resid_in.reshape(samples * node_count, feat_width) + attn_sum
    normed2 = layer_norm(residual.reshape(samples, node_count, feat_width), norm_gain[1][:, None, :], norm_shift[1][:, None, :]).astype(jnp.bfloat16)
    normed2 = normed2.reshape(samples * node_count, feat_width)
    hidden = jax.nn.silu(jnp.dot(normed2, up_weight, preferred_element_type=jnp.float32)).astype(jnp.bfloat16)
    update = jnp.zeros((samples * node_count, feat_width), jnp.float32)
    for tp_rank in range(N_TP):
        unit_first = tp_rank * unit_cols
        term_part = jnp.dot(hidden[:, unit_first:unit_first + unit_cols], down_weight[unit_first:unit_first + unit_cols], preferred_element_type=jnp.float32).astype(jnp.bfloat16)
        term_part = lax.optimization_barrier(term_part)
        update = update + term_part.astype(jnp.float32)
    return (residual + update).astype(jnp.bfloat16).reshape(samples, node_count, feat_width)
```

```python
import math

import jax
import jax.numpy as jnp
from jax import lax
from jax.experimental import pallas as pl
from jax.experimental.pallas import tpu as pltpu
from jax.sharding import PartitionSpec as P

HEADS = 4
NODE_BLK = 128
KMAX = 8
FAR = 3


def layer_norm(values, gain_row, shift_row):
    row_mean = jnp.mean(values, axis=-1, keepdims=True)
    centred = values - row_mean
    spread = jnp.mean(centred * centred, axis=-1, keepdims=True)
    return centred * lax.rsqrt(spread + 1e-05) * gain_row + shift_row


def layer_kernel(
    slots, live, state, gain, shift, wqkv, wout, wup, wdown, out,
    nrm, kv, query, heads, outgoing, wout_all, wup_all, wdown_all, resid, normed2, total, cols,
    z_s, z_r, y_s, y_r, a_s, a_r, b_s, b_r, n_s, n_r, m_s, m_r, wy_s, wy_r, wa_s, wa_r, wb_s, wb_r,
    h_s, h_r, o_s, o_r,
):
    d = lax.axis_index("dom")
    t = lax.axis_index("tp")
    doms = lax.axis_size("dom")
    odd = lax.rem(d, 2)
    near = d + 1 - 2 * odd
    diag = lax.rem(d - 1 + 2 * odd + doms, doms)
    plus = lax.rem(d + 2, doms)
    minus = lax.rem(d + doms - 2, doms)
    core = lax.rem(t, 2)
    sib = t + 1 - 2 * core
    across = lax.rem(t + 2, 4)
    corner = lax.rem(sib + 2, 4)
    targets = (diag, minus, plus)
    f32 = jnp.float32

    def remote(src, dst, send, recv, dd, tt):
        return pltpu.make_async_remote_copy(
            src_ref=src, dst_ref=dst, send_sem=send, recv_sem=recv, device_id=(dd, tt),
            device_id_type=pl.DeviceIdType.MESH,
        )

    barrier = pltpu.get_barrier_semaphore()
    partners = [(near, t), (diag, t), (plus, t), (minus, t), (d, sib), (d, across), (d, corner)]
    for partner in partners:
        pl.semaphore_signal(
            barrier, inc=1, device_id=partner, device_id_type=pl.DeviceIdType.MESH
        )

    def norm_one(u, carry):
        s = u // 8
        nrm[u] = layer_norm(state[u].astype(f32), gain[0, s], shift[0, s]).astype(jnp.bfloat16)
        return carry

    lax.fori_loop(0, 16, norm_one, 0)
    pl.semaphore_wait(barrier, 7)

    def z_copy(f, i):
        return remote(
            nrm.at[4 * t + i], nrm.at[(2 + f) * 16 + 4 * t + i], z_s.at[f, i], z_r.at[f, i],
            targets[f], t,
        )

    def y_copy(f, i, owner=t):
        u = (2 + f) * 16 + 4 * owner + i
        return remote(nrm.at[u], nrm.at[u], y_s.at[f, i], y_r.at[f, i], d, across)

    def a_copy(f, i, owner=t):
        u = (2 + f) * 16 + 4 * owner + i
        return remote(nrm.at[u], nrm.at[u], a_s.at[f, i], a_r.at[f, i], d, sib)

    def b_copy(f, i, owner=across):
        u = (2 + f) * 16 + 4 * owner + i
        return remote(nrm.at[u], nrm.at[u], b_s.at[f, i], b_r.at[f, i], d, sib)

    def n_copy(i):
        u = 8 * core + 2 * i
        return remote(
            nrm.at[pl.ds(u, 2)], nrm.at[pl.ds(16 + u, 2)], n_s.at[i], n_r.at[i], near, t
        )

    def m_copy(i, side=core):
        u = 16 + 8 * side + 2 * i
        return remote(nrm.at[pl.ds(u, 2)], nrm.at[pl.ds(u, 2)], m_s.at[i], m_r.at[i], d, sib)

    shards = ((wout, wout_all), (wup, wup_all), (wdown, wdown_all))

    def wy_copy(k, owner=t):
        return remote(shards[k][0], shards[k][1].at[owner], wy_s.at[k], wy_r.at[k], d, across)

    def wa_copy(k, owner=t):
        return remote(shards[k][0], shards[k][1].at[owner], wa_s.at[k], wa_r.at[k], d, sib)

    def wb_copy(k, owner=across):
        full = shards[k][1]
        return remote(full.at[owner], full.at[owner], wb_s.at[k], wb_r.at[k], d, sib)

    def send_all(i, carry):
        for f in range(FAR):
            z_copy(f, i).start()
        n_copy(i).start()
        return carry

    lax.fori_loop(0, 4, send_all, 0)
    for k in range(3):
        wa_copy(k).start()
    for shard, full in shards:
        full[t] = shard[...]

    def project_own(u, carry):
        made = jnp.dot(nrm[u], wqkv[...], preferred_element_type=f32).astype(jnp.bfloat16)
        query[u] = made[:, :128]
        kv[u] = made[:, 128:]
        return carry

    lax.fori_loop(0, 16, project_own, 0)

    def project(u):
        kv[u] = jnp.dot(nrm[u], wqkv[:, 128:], preferred_element_type=f32).astype(jnp.bfloat16)

    def relay(i, carry):
        @pl.when(i < 4)
        def _():
            for f in range(FAR):
                z_copy(f, i).wait_recv()
                y_copy(f, i).start()
                a_copy(f, i).start()
            n_copy(i).wait_recv()
            m_copy(i).start()
            for f in range(FAR):
                project((2 + f) * 16 + 4 * t + i)

        @pl.when(i > 0)
        def _():
            for f in range(FAR):
                y_copy(f, i - 1, across).wait_recv()
                b_copy(f, i - 1).start()
            for f in range(FAR):
                project((2 + f) * 16 + 4 * across + i - 1)

        return carry

    lax.fori_loop(0, 5, relay, 0)
    for k in range(3):
        wy_copy(k).start()

    def take_sib(i, carry):
        for f in range(FAR):
            a_copy(f, i, sib).wait_recv()
        m_copy(i, 1 - core).wait_recv()
        for f in range(FAR):
            project((2 + f) * 16 + 4 * sib + i)
        for r in range(2):
            project(16 + 8 * core + 2 * i + r)
            project(16 + 8 * (1 - core) + 2 * i + r)
        return carry

    lax.fori_loop(0, 4, take_sib, 0)

    def take_corner(i, carry):
        for f in range(FAR):
            b_copy(f, i, corner).wait_recv()
        for f in range(FAR):
            project((2 + f) * 16 + 4 * corner + i)
        return carry

    lax.fori_loop(0, 4, take_corner, 0)

    scale = 1.0 / math.sqrt(128)
    lane_entry = lax.broadcasted_iota(jnp.int32, (1, KMAX * NODE_BLK), 1) // NODE_BLK

    def attend(b, s):
        q = query[s * 8 + b]
        places = [slots[b, j] + s * 8 for j in range(KMAX)]
        scores = jnp.concatenate(
            [
                lax.dot_general(
                    q, kv[places[j], :, :128], (((1,), (1,)), ((), ())),
                    preferred_element_type=f32,
                )
                for j in range(KMAX)
            ],
            axis=1,
        )
        scores = jnp.where(lane_entry < live[b], scores, -1e30)
        top = jnp.max(scores, axis=1, keepdims=True)
        weights = jnp.exp((scores - top) * scale)
        whole = jnp.sum(weights, axis=1, keepdims=True)
        weights = weights.astype(jnp.bfloat16)
        mixed = jnp.zeros((NODE_BLK, 128), f32)
        for j in range(KMAX):
            mixed += jnp.dot(
                weights[:, j * 128 : (j + 1) * 128], kv[places[j], :, 128:],
                preferred_element_type=f32,
            )
        return (mixed / whole).astype(jnp.bfloat16)

    def h_copy(k, src_tp=t):
        owner = lax.rem(t + 1 + k // 2, 4)
        place = lax.rem(k, 2) * 256
        return remote(
            outgoing.at[k], heads.at[src_tp, pl.ds(place, 256)], h_s.at[k], h_r.at[k], d, owner
        )

    def attend_away(k, carry):
        b = lax.rem(2 * (t + 1) + k, 8)
        for s in range(2):
            outgoing[k, s * 128 : (s + 1) * 128] = attend(b, s)
        h_copy(k).start()
        return carry

    lax.fori_loop(0, 6, attend_away, 0)

    def attend_here(r, carry):
        for s in range(2):
            heads[t, pl.ds(pl.multiple_of(r * 256 + s * 128, 128), 128)] = attend(2 * t + r, s)
        return carry

    lax.fori_loop(0, 2, attend_here, 0)

    for k in range(3):
        wy_copy(k, across).wait_recv()
        wb_copy(k).start()
    for k in range(6):
        h_copy(k, lax.rem(t + 3 - k // 2, 4)).wait_recv()
    wa_copy(0, sib).wait_recv()
    wb_copy(0, corner).wait_recv()

    for lu in range(4):
        r, s = lu // 2, lu % 2
        rows = slice(lu * 128, (lu + 1) * 128)
        attn = jnp.zeros((128, 512), f32)
        for h in range(HEADS):
            attn += (
                jnp.dot(heads[h, rows], wout_all[h], preferred_element_type=f32)
                .astype(jnp.bfloat16)
                .astype(f32)
            )
        after = state[s * 8 + 2 * t + r].astype(f32) + attn
        resid[rows] = after
        normed2[rows] = layer_norm(after, gain[1, s], shift[1, s]).astype(jnp.bfloat16)
    total[...] = jnp.zeros_like(total)

    def mlp(g):
        for half in range(2):
            rows = slice(half * 256, (half + 1) * 256)
            pre = jnp.dot(normed2[rows], wup_all[g], preferred_element_type=f32)
            hidden = (pre / (1.0 + jnp.exp(-pre))).astype(jnp.bfloat16)
            term = jnp.dot(hidden, wdown_all[g], preferred_element_type=f32)
            total[rows] += term.astype(jnp.bfloat16).astype(f32)

    wa_copy(1, sib).wait_recv()
    wa_copy(2, sib).wait_recv()
    lax.fori_loop(0, 2, lambda k, c: (mlp(t - core + k), c)[1], 0)
    wb_copy(1, corner).wait_recv()
    wb_copy(2, corner).wait_recv()
    lax.fori_loop(0, 2, lambda k, c: (mlp(across - core + k), c)[1], 0)

    for j in range(4):
        lanes = slice(j * 128, (j + 1) * 128)
        cols[j] = (resid[:, lanes] + total[:, lanes]).astype(jnp.bfloat16)

    def o_copy(k, owner=t):
        peer = lax.rem(t + 1 + k, 4)
        return remote(cols.at[peer], out.at[owner], o_s.at[k], o_r.at[k], d, peer)

    for k in range(3):
        o_copy(k).start()
    out[t] = cols[t]
    for k in range(3):
        o_copy(k, lax.rem(t + 3 - k, 4)).wait_recv()

    def drain(i, carry):
        for f in range(FAR):
            z_copy(f, i).wait_send()
            y_copy(f, i).wait_send()
            a_copy(f, i).wait_send()
            b_copy(f, i).wait_send()
        n_copy(i).wait_send()
        m_copy(i).wait_send()
        return carry

    lax.fori_loop(0, 4, drain, 0)
    for k in range(3):
        wy_copy(k).wait_send()
        wa_copy(k).wait_send()
        wb_copy(k).wait_send()
        o_copy(k).wait_send()
    for k in range(6):
        h_copy(k).wait_send()


def local(
    state, norm_gain, norm_shift, qkv_weight, out_weight, up_weight, down_weight, neighbours, counts
):
    samples, row_count, feat = state.shape
    per_dev = row_count // NODE_BLK
    doms = lax.axis_size("dom")
    d = lax.axis_index("dom")
    odd = d % 2
    away = jnp.mod(neighbours // per_dev - d, doms)
    slot = jnp.where(away == 0, 0, 0)
    slot = jnp.where(away == 1, 1 + odd, slot)
    slot = jnp.where(away == doms - 1, 2 - odd, slot)
    slot = jnp.where(away == 2, 3, slot)
    slot = jnp.where(away == doms - 2, 4, slot)
    slots = (slot * 16 + neighbours % per_dev).astype(jnp.int32)
    bf16 = jnp.bfloat16
    dma = pltpu.SemaphoreType.DMA
    smem = pl.BlockSpec(memory_space=pltpu.SMEM)
    vmem = pl.BlockSpec(memory_space=pltpu.VMEM)
    pairs = []
    for shape in [(3, 4)] * 4 + [(4,)] * 2 + [(3,)] * 3 + [(6,), (3,)]:
        pairs += [dma(shape), dma(shape)]
    out = pl.pallas_call(
        layer_kernel,
        out_shape=jax.ShapeDtypeStruct((4, 512, 128), bf16),
        in_specs=[smem, smem] + [vmem] * 7,
        out_specs=vmem,
        scratch_shapes=[
            pltpu.VMEM((80, 128, 512), bf16),
            pltpu.VMEM((80, 128, 256), bf16),
            pltpu.VMEM((16, 128, 128), bf16),
            pltpu.VMEM((4, 512, 128), bf16),
            pltpu.VMEM((6, 256, 128), bf16),
            pltpu.VMEM((4, 128, 512), bf16),
            pltpu.VMEM((4, 512, 512), bf16),
            pltpu.VMEM((4, 512, 512), bf16),
            pltpu.VMEM((512, 512), jnp.float32),
            pltpu.VMEM((512, 512), bf16),
            pltpu.VMEM((512, 512), jnp.float32),
            pltpu.VMEM((4, 512, 128), bf16),
        ]
        + pairs,
        compiler_params=pltpu.CompilerParams(
            collective_id=0, has_side_effects=True, vmem_limit_bytes=50 * 2**20
        ),
    )(
        slots,
        counts,
        state.reshape(samples * per_dev, NODE_BLK, feat),
        norm_gain.reshape(2, 2, 1, feat),
        norm_shift.reshape(2, 2, 1, feat),
        qkv_weight.reshape(feat, -1),
        out_weight,
        up_weight,
        down_weight,
    )
    out = out.reshape(per_dev, samples, NODE_BLK, 128)
    return jnp.transpose(out, (1, 0, 2, 3)).reshape(samples, row_count, 128)


def solution(mesh):
    placed = (
        P(None, "dom", None),
        P(),
        P(),
        P(None, None, "tp"),
        P("tp", None),
        P(None, "tp"),
        P("tp", None),
        P("dom", None),
        P("dom"),
    )
    return jax.shard_map(
        local, mesh=mesh, in_specs=placed, out_specs=P(None, "dom", "tp"), check_vma=False
    )
```

```python
import math

import jax
import jax.numpy as jnp
from jax import lax
from jax.experimental import pallas as pl
from jax.experimental.pallas import tpu as pltpu
from jax.sharding import PartitionSpec as P

HEADS = 4
NODE_BLK = 128
KMAX = 8
FLOWS = 3


def layer_norm(values, gain_row, shift_row):
    row_mean = jnp.mean(values, axis=-1, keepdims=True)
    centred = values - row_mean
    spread = jnp.mean(centred * centred, axis=-1, keepdims=True)
    return centred * lax.rsqrt(spread + 1e-05) * gain_row + shift_row


def layer_kernel(
    neigh, live, gain, shift, state_in, wqkv_in, wout_in, wup_in, wdown_in, out,
    state, wqkv_raw, wqkv, nrm, kv, query, heads, outgoing, wout_all, wup_all, wdown_all, normed2,
    cols, c_state, c_w,
    z_s, z_r, y_s, y_r, a_s, a_r, b_s, b_r, x_s, x_r, n_s, n_r, m_s, m_r,
    wy_s, wy_r, wa_s, wa_r, wx_s, wx_r, w0_s, w0_r, w1_s, w1_r, h_s, h_r, o_s, o_r,
):
    d = lax.axis_index("dom")
    t = lax.axis_index("tp")
    doms = lax.axis_size("dom")
    odd = lax.rem(d, 2)
    near = d + 1 - 2 * odd
    plus = lax.rem(d + 2, doms)
    minus = lax.rem(d + doms - 2, doms)
    core = lax.rem(t, 2)
    sib = t + 1 - 2 * core
    across = lax.rem(t + 2, 4)
    corner = lax.rem(sib + 2, 4)
    f32 = jnp.float32
    bf16 = jnp.bfloat16

    def remote(src, dst, send, recv, dd, tt):
        return pltpu.make_async_remote_copy(
            src_ref=src, dst_ref=dst, send_sem=send, recv_sem=recv, device_id=(dd, tt),
            device_id_type=pl.DeviceIdType.MESH,
        )

    barrier = pltpu.get_barrier_semaphore()
    for partner in [(near, t), (plus, t), (minus, t), (d, sib), (d, across), (d, corner)]:
        pl.semaphore_signal(
            barrier, inc=1, device_id=partner, device_id_type=pl.DeviceIdType.MESH
        )

    def state_copy(k):
        rows = pl.ds(4 * lax.rem(t + k, 4), 4)
        return pltpu.make_async_copy(state_in.at[rows], state.at[rows], c_state.at[k])

    shards = ((wout_in, wout_all), (wup_in, wup_all), (wdown_in, wdown_all))
    own_copies = [pltpu.make_async_copy(wqkv_in, wqkv_raw, c_w.at[3])] + [
        pltpu.make_async_copy(shard, full.at[t], c_w.at[k])
        for k, (shard, full) in enumerate(shards)
    ]
    for k in range(4):
        state_copy(k).start()
    for copy in own_copies:
        copy.start()

    def norm_quarter(k, carry):
        state_copy(k).wait()

        def norm_one(i, inner):
            u = 4 * lax.rem(t + k, 4) + i
            s = u // 8
            nrm[u] = layer_norm(
                state[u].astype(f32), gain[0, pl.ds(s, 1)], shift[0, pl.ds(s, 1)]
            ).astype(bf16)
            return inner

        lax.fori_loop(0, 4, norm_one, 0)
        return carry

    def z_copy(f, i):
        return remote(
            nrm.at[4 * t + i], nrm.at[(2 + f) * 16 + 4 * t + i], z_s.at[f - 1, i],
            z_r.at[f - 1, i], (minus, plus)[f - 1], t,
        )

    def x_copy(i):
        u = 4 * t + i
        return remote(
            nrm.at[(3 + odd) * 16 + u], nrm.at[2 * 16 + u], x_s.at[i], x_r.at[i], near, t
        )

    def y_copy(f, i, owner=t):
        u = (2 + f) * 16 + 4 * owner + i
        return remote(nrm.at[u], nrm.at[u], y_s.at[f, i], y_r.at[f, i], d, across)

    def a_copy(f, i, owner=t):
        u = (2 + f) * 16 + 4 * owner + i
        return remote(nrm.at[u], nrm.at[u], a_s.at[f, i], a_r.at[f, i], d, sib)

    def b_copy(f, i, owner=across):
        u = (2 + f) * 16 + 4 * owner + i
        return remote(nrm.at[u], nrm.at[u], b_s.at[f, i], b_r.at[f, i], d, sib)

    def n_copy(i):
        u = 8 * core + 2 * i
        return remote(
            nrm.at[pl.ds(u, 2)], nrm.at[pl.ds(16 + u, 2)], n_s.at[i], n_r.at[i], near, t
        )

    def m_copy(i, side=core):
        u = 16 + 8 * side + 2 * i
        return remote(nrm.at[pl.ds(u, 2)], nrm.at[pl.ds(u, 2)], m_s.at[i], m_r.at[i], d, sib)

    def part(k, owner, half):
        rows = shards[k][0].shape[0] // 2
        return shards[k][1].at[owner, pl.ds(pl.multiple_of(half * rows, 64), rows)]

    def wa_copy(k, owner=t):
        full = shards[k][1]
        return remote(full.at[owner], full.at[owner], wa_s.at[k], wa_r.at[k], d, sib)

    def wy_copy(k, owner=t):
        ref = part(k, owner, odd)
        return remote(ref, ref, wy_s.at[k], wy_r.at[k], d, across)

    def wx_copy(k, half=odd):
        ref = part(k, across, half)
        return remote(ref, ref, wx_s.at[k], wx_r.at[k], near, t)

    def w0_copy(k, owner=across):
        ref = part(k, owner, odd)
        return remote(ref, ref, w0_s.at[k], w0_r.at[k], d, sib)

    def w1_copy(k, owner=across):
        ref = part(k, owner, 1 - odd)
        return remote(ref, ref, w1_s.at[k], w1_r.at[k], d, sib)

    norm_quarter(0, 0)
    pl.semaphore_wait(barrier, 6)
    for i in range(4):
        for f in (1, 2):
            z_copy(f, i).start()
    lax.fori_loop(1, 4, norm_quarter, 0)
    n_copy(0).start()

    for copy in own_copies:
        copy.wait()
    for k in range(3):
        wa_copy(k).start()
    for c in range(3):
        wqkv[:, c * 128 : (c + 1) * 128] = wqkv_raw[c]

    def project_own(k, carry):
        rows = pl.ds(4 * k, 4)
        made = jnp.dot(
            nrm[rows].reshape(512, 512), wqkv[...], preferred_element_type=f32
        ).astype(bf16)
        query[rows] = made[:, :128].reshape(4, 128, 128)
        kv[rows] = made[:, 128:].reshape(4, 128, 256)
        return carry

    lax.fori_loop(0, 4, project_own, 0)

    def project(slot, quarter):
        rows = pl.ds(slot * 16 + 4 * quarter, 4)
        kv[rows] = (
            jnp.dot(nrm[rows].reshape(512, 512), wqkv[:, 128:], preferred_element_type=f32)
            .astype(bf16)
            .reshape(4, 128, 256)
        )

    def project_flows(quarter):
        lax.fori_loop(0, FLOWS, lambda f, c: (project(2 + f, quarter), c)[1], 0)

    def relay(i, carry):
        @pl.when(i < 4)
        def _():
            for f in (1, 2):
                z_copy(f, i).wait_recv()
            x_copy(i).start()
            for f in (1, 2):
                y_copy(f, i).start()
                a_copy(f, i).start()

        @pl.when(i < 3)
        def _():
            n_copy(i + 1).start()

        @pl.when((i > 0) & (i < 5))
        def _():
            n_copy(i - 1).wait_recv()
            m_copy(i - 1).start()
            x_copy(i - 1).wait_recv()
            y_copy(0, i - 1).start()
            a_copy(0, i - 1).start()

        @pl.when(i == 5)
        def _():
            for k in range(3):
                wy_copy(k).start()
            project_flows(t)
            project(1, 2 * core)
            project(1, 2 * core + 1)

        @pl.when(i > 1)
        def _():
            for f in range(FLOWS):
                y_copy(f, i - 2, across).wait_recv()
                b_copy(f, i - 2).start()

        return carry

    lax.fori_loop(0, 6, relay, 0)
    project_flows(across)
    for i in range(4):
        for f in range(FLOWS):
            a_copy(f, i, sib).wait_recv()
        m_copy(i, 1 - core).wait_recv()
    project_flows(sib)
    project(1, 2 - 2 * core)
    project(1, 3 - 2 * core)
    for i in range(4):
        for f in range(FLOWS):
            b_copy(f, i, corner).wait_recv()
    project_flows(corner)

    scale = 1.0 / math.sqrt(128)
    lane_entry = lax.broadcasted_iota(jnp.int32, (1, KMAX * NODE_BLK), 1) // NODE_BLK

    def place_of(b, j):
        block = neigh[b, j]
        away = lax.rem(lax.div(block, 8) - d + doms, doms)
        slot = jnp.where(away == 1, 1 + odd, 0)
        slot = jnp.where(away == doms - 1, 2 - odd, slot)
        slot = jnp.where(away == 2, 3, slot)
        slot = jnp.where(away == doms - 2, 4, slot)
        return slot * 16 + lax.rem(block, 8)

    def attend(b):
        firsts = [place_of(b, j) for j in range(KMAX)]
        made = []
        for s in range(2):
            q = query[s * 8 + b]
            scores = jnp.concatenate(
                [
                    lax.dot_general(
                        q, kv[first + s * 8, :, :128], (((1,), (1,)), ((), ())),
                        preferred_element_type=f32,
                    )
                    for first in firsts
                ],
                axis=1,
            )
            scores = jnp.where(lane_entry < live[b], scores, -1e30)
            top = jnp.max(scores, axis=1, keepdims=True)
            weights = jnp.exp((scores - top) * scale)
            whole = jnp.sum(weights, axis=1, keepdims=True)
            weights = weights.astype(bf16)
            mixed = jnp.zeros((NODE_BLK, 128), f32)
            for j, first in enumerate(firsts):
                mixed += jnp.dot(
                    weights[:, j * 128 : (j + 1) * 128], kv[first + s * 8, :, 128:],
                    preferred_element_type=f32,
                )
            made.append((mixed / whole).astype(bf16))
        return jnp.concatenate(made, axis=0)

    def h_copy(k, src_tp=t):
        owner = lax.rem(t + 1 + k // 2, 4)
        place = lax.rem(k, 2) * 256
        return remote(
            outgoing.at[k], heads.at[src_tp, pl.ds(place, 256)], h_s.at[k], h_r.at[k], d, owner
        )

    def attend_away(k, carry):
        for step, ready in ((2, (0, 1)), (4, (2,))):

            @pl.when(k == step)
            def _():
                for w in ready:
                    wy_copy(w, across).wait_recv()
                    wx_copy(w).start()
                    w0_copy(w).start()

        outgoing[k] = attend(lax.rem(2 * (t + 1) + k, 8))
        h_copy(k).start()
        return carry

    lax.fori_loop(0, 6, attend_away, 0)
    for w in range(2):
        wx_copy(w, 1 - odd).wait_recv()
        w1_copy(w).start()

    def attend_here(r, carry):
        heads[t, pl.ds(pl.multiple_of(r * 256, 256), 256)] = attend(2 * t + r)
        return carry

    lax.fori_loop(0, 2, attend_here, 0)

    wx_copy(2, 1 - odd).wait_recv()
    w1_copy(2).start()
    for k in range(6):
        h_copy(k, lax.rem(t + 3 - k // 2, 4)).wait_recv()
    for k in range(3):
        wa_copy(k, sib).wait_recv()
        w0_copy(k, corner).wait_recv()
        w1_copy(k, corner).wait_recv()

    def o_copy(k, r, owner=t):
        peer = lax.rem(t + 1 + k, 4)
        rows = pl.ds(pl.multiple_of(r * 256, 256), 256)
        return remote(
            cols.at[peer, rows], out.at[owner, rows], o_s.at[k, r], o_r.at[k, r], d, peer
        )

    def finish(r, carry):
        rows = pl.ds(pl.multiple_of(r * 256, 256), 256)
        attn = jnp.zeros((256, 512), f32)
        for h in range(HEADS):
            attn += (
                jnp.dot(heads[h, rows], wout_all[h], preferred_element_type=f32)
                .astype(bf16)
                .astype(f32)
            )
        after = []
        for s in range(2):
            after.append(
                state[s * 8 + 2 * t + r].astype(f32) + attn[s * 128 : (s + 1) * 128]
            )
            normed2[s * 128 : (s + 1) * 128] = layer_norm(
                after[s], gain[1, s : s + 1], shift[1, s : s + 1]
            ).astype(bf16)

        def hidden_group(g, total):
            pre = jnp.dot(normed2[...], wup_all[g], preferred_element_type=f32)
            hidden = (0.5 * pre * (1.0 + jnp.tanh(0.5 * pre))).astype(bf16)
            term = jnp.dot(hidden, wdown_all[g], preferred_element_type=f32)
            return total + term.astype(bf16).astype(f32)

        total = lax.fori_loop(0, 4, hidden_group, jnp.concatenate(after, axis=0))
        for j in range(4):
            cols[j, rows] = total[:, j * 128 : (j + 1) * 128].astype(bf16)
        for k in range(3):
            o_copy(k, r).start()
        out[t, rows] = cols[t, rows]
        return carry

    lax.fori_loop(0, 2, finish, 0)

    def drain(i, carry):
        for f in (1, 2):
            z_copy(f, i).wait_send()
        for f in range(FLOWS):
            y_copy(f, i).wait_send()
            a_copy(f, i).wait_send()
            b_copy(f, i).wait_send()
        x_copy(i).wait_send()
        n_copy(i).wait_send()
        m_copy(i).wait_send()
        return carry

    lax.fori_loop(0, 4, drain, 0)
    for k in range(3):
        for copy in (wy_copy, wa_copy, wx_copy, w0_copy, w1_copy):
            copy(k).wait_send()
    for k in range(6):
        h_copy(k).wait_send()
    for r in range(2):
        for k in range(3):
            o_copy(k, r, lax.rem(t + 3 - k, 4)).wait_recv()
            o_copy(k, r).wait_send()


def local(
    state, norm_gain, norm_shift, qkv_weight, out_weight, up_weight, down_weight, neighbours, counts
):
    samples, row_count, feat = state.shape
    per_dev = row_count // NODE_BLK
    bf16 = jnp.bfloat16
    dma = pltpu.SemaphoreType.DMA
    smem = pl.BlockSpec(memory_space=pltpu.SMEM)
    vmem = pl.BlockSpec(memory_space=pltpu.VMEM)
    anywhere = pl.BlockSpec(memory_space=pl.ANY)
    pairs = [dma((4,)), dma((4,))]
    for shape in [(2, 4)] + [(3, 4)] * 3 + [(4,)] * 3 + [(3,)] * 5 + [(6,), (3, 2)]:
        pairs += [dma(shape), dma(shape)]
    out = pl.pallas_call(
        layer_kernel,
        out_shape=jax.ShapeDtypeStruct((4, 512, 128), bf16),
        in_specs=[smem, smem, vmem, vmem] + [anywhere] * 5,
        out_specs=vmem,
        scratch_shapes=[
            pltpu.VMEM((16, 128, 512), bf16),
            pltpu.VMEM((3, 512, 128), bf16),
            pltpu.VMEM((512, 384), bf16),
            pltpu.VMEM((80, 128, 512), bf16),
            pltpu.VMEM((80, 128, 256), bf16),
            pltpu.VMEM((16, 128, 128), bf16),
            pltpu.VMEM((4, 512, 128), bf16),
            pltpu.VMEM((6, 256, 128), bf16),
            pltpu.VMEM((4, 128, 512), bf16),
            pltpu.VMEM((4, 512, 512), bf16),
            pltpu.VMEM((4, 512, 512), bf16),
            pltpu.VMEM((256, 512), bf16),
            pltpu.VMEM((4, 512, 128), bf16),
        ]
        + pairs,
        compiler_params=pltpu.CompilerParams(
            collective_id=0, has_side_effects=True, vmem_limit_bytes=62 * 2**20
        ),
    )(
        neighbours,
        counts,
        norm_gain,
        norm_shift,
        state.reshape(samples * per_dev, NODE_BLK, feat),
        jnp.transpose(qkv_weight, (1, 0, 2)),
        out_weight,
        up_weight,
        down_weight,
    )
    out = out.reshape(per_dev, samples, NODE_BLK, 128)
    return jnp.transpose(out, (1, 0, 2, 3)).reshape(samples, row_count, 128)


def solution(mesh):
    placed = (
        P(None, "dom", None),
        P(),
        P(),
        P(None, None, "tp"),
        P("tp", None),
        P(None, "tp"),
        P("tp", None),
        P("dom", None),
        P("dom"),
    )
    return jax.shard_map(
        local, mesh=mesh, in_specs=placed, out_specs=P(None, "dom", "tp"), check_vma=False
    )
```

```python
import math

import jax
import jax.numpy as jnp
from jax import lax
from jax.experimental import pallas as pl
from jax.experimental.pallas import tpu as pltpu
from jax.sharding import PartitionSpec as P

HEADS = 4
NODE_BLK = 128
KMAX = 8


def layer_norm(values, gain_row, shift_row):
    row_mean = jnp.mean(values, axis=-1, keepdims=True)
    centred = values - row_mean
    spread = jnp.mean(centred * centred, axis=-1, keepdims=True)
    return centred * lax.rsqrt(spread + 1e-05) * gain_row + shift_row


def layer_kernel(
    neigh, live, gain, shift, state_in, wqkv_in, wout_in, wup_in, wdown_in, out,
    state, wqkv_raw, wqkv, nrm, kv, query, heads, outgoing, wout_all, wup_all, wdown_all, normed2,
    cols, c_state, c_w,
    z_s, z_r, y_s, y_r, a_s, a_r, b_s, b_r, x_s, x_r, n_s, n_r, m_s, m_r,
    wy_s, wy_r, wa_s, wa_r, wx_s, wx_r, w0_s, w0_r, w1_s, w1_r, h_s, h_r, o_s, o_r,
):
    d = lax.axis_index("dom")
    t = lax.axis_index("tp")
    doms = lax.axis_size("dom")
    odd = lax.rem(d, 2)
    near = d + 1 - 2 * odd
    plus = lax.rem(d + 2, doms)
    minus = lax.rem(d + doms - 2, doms)
    core = lax.rem(t, 2)
    sib = t + 1 - 2 * core
    across = lax.rem(t + 2, 4)
    corner = lax.rem(sib + 2, 4)
    f32 = jnp.float32
    bf16 = jnp.bfloat16

    def remote(src, dst, send, recv, dd, tt):
        return pltpu.make_async_remote_copy(
            src_ref=src, dst_ref=dst, send_sem=send, recv_sem=recv, device_id=(dd, tt),
            device_id_type=pl.DeviceIdType.MESH,
        )

    barrier = pltpu.get_barrier_semaphore()
    for partner in [(near, t), (plus, t), (minus, t), (d, sib), (d, across), (d, corner)]:
        pl.semaphore_signal(
            barrier, inc=1, device_id=partner, device_id_type=pl.DeviceIdType.MESH
        )

    def state_copy(s):
        rows = pl.ds(8 * s, 8)
        return pltpu.make_async_copy(state_in.at[rows], state.at[rows], c_state.at[s])

    shards = ((wout_in, wout_all), (wup_in, wup_all), (wdown_in, wdown_all))
    own_copies = [pltpu.make_async_copy(wqkv_in, wqkv_raw, c_w.at[3])] + [
        pltpu.make_async_copy(shard, full.at[t], c_w.at[k])
        for k, (shard, full) in enumerate(shards)
    ]
    for s in range(2):
        state_copy(s).start()
    for copy in own_copies:
        copy.start()

    def norm_units(s, first, count, around=8):
        def norm_one(i, inner):
            u = 8 * s + lax.rem(first + i, around)
            nrm[u] = layer_norm(
                state[u].astype(f32), gain[0, s : s + 1], shift[0, s : s + 1]
            ).astype(bf16)
            return inner

        lax.fori_loop(0, count, norm_one, 0)

    def unit(rank, j):
        side = lax.div(rank, 2)
        shared = 4 + 2 * lax.rem(rank, 2)
        return (rank, shared + side, shared + 1 - side)[j]

    def z_copy(f, s, j):
        u = 8 * s + unit(t, j)
        return remote(
            nrm.at[u], nrm.at[(2 + f) * 16 + u], z_s.at[f - 1, 3 * s + j],
            z_r.at[f - 1, 3 * s + j], (minus, plus)[f - 1], t,
        )

    def x_copy(s, j):
        u = 8 * s + unit(t, j)
        k = 2 * s + j
        return remote(
            nrm.at[(3 + odd) * 16 + u], nrm.at[2 * 16 + u], x_s.at[k], x_r.at[k], near, t
        )

    def y_copy(f, s, j, owner=t):
        u = (2 + f) * 16 + 8 * s + unit(owner, j)
        k = 2 * s + j
        return remote(nrm.at[u], nrm.at[u], y_s.at[f, k], y_r.at[f, k], d, across)

    def a_copy(f, s, j, owner=t):
        u = (2 + f) * 16 + 8 * s + unit(owner, j)
        k = 3 * s + j
        return remote(nrm.at[u], nrm.at[u], a_s.at[f, k], a_r.at[f, k], d, sib)

    def b_copy(f, s, j, owner=across):
        u = (2 + f) * 16 + 8 * s + unit(owner, j)
        k = 2 * s + j
        return remote(nrm.at[u], nrm.at[u], b_s.at[f, k], b_r.at[f, k], d, sib)

    def n_copy(i):
        u = 8 * (i // 2) + 4 * core + 2 * (i % 2)
        return remote(
            nrm.at[pl.ds(u, 2)], nrm.at[pl.ds(16 + u, 2)], n_s.at[i], n_r.at[i], near, t
        )

    def m_copy(i, side=core):
        u = 16 + 8 * (i // 2) + 4 * side + 2 * (i % 2)
        return remote(nrm.at[pl.ds(u, 2)], nrm.at[pl.ds(u, 2)], m_s.at[i], m_r.at[i], d, sib)

    def part(k, owner, half):
        rows = shards[k][0].shape[0] // 2
        return shards[k][1].at[owner, pl.ds(pl.multiple_of(half * rows, 64), rows)]

    def wa_copy(k, owner=t):
        full = shards[k][1]
        return remote(full.at[owner], full.at[owner], wa_s.at[k], wa_r.at[k], d, sib)

    def wy_copy(k, owner=t):
        ref = part(k, owner, odd)
        return remote(ref, ref, wy_s.at[k], wy_r.at[k], d, across)

    def wx_copy(k, half=odd):
        ref = part(k, across, half)
        return remote(ref, ref, wx_s.at[k], wx_r.at[k], near, t)

    def w0_copy(k, owner=across):
        ref = part(k, owner, odd)
        return remote(ref, ref, w0_s.at[k], w0_r.at[k], d, sib)

    def w1_copy(k, owner=across):
        ref = part(k, owner, 1 - odd)
        return remote(ref, ref, w1_s.at[k], w1_r.at[k], d, sib)

    state_copy(0).wait()
    norm_units(0, t, 1)
    norm_units(0, 4 + 2 * core, 2)
    pl.semaphore_wait(barrier, 6)
    for j in range(3):
        for f in (1, 2):
            z_copy(f, 0, j).start()
    norm_units(0, t + 1, 3, 4)
    norm_units(0, 6 - 2 * core, 2)
    n_copy(0).start()
    n_copy(1).start()
    for copy in own_copies:
        copy.wait()
    for k in range(2):
        wy_copy(k).start()
    state_copy(1).wait()
    norm_units(1, 0, 8)
    for j in range(3):
        for f in (1, 2):
            z_copy(f, 1, j).start()
    for k in range(3):
        wa_copy(k).start()
    for c in range(3):
        wqkv[:, c * 128 : (c + 1) * 128] = wqkv_raw[c]

    def project_own(k, carry):
        rows = pl.ds(4 * k, 4)
        made = jnp.dot(
            nrm[rows].reshape(512, 512), wqkv[...], preferred_element_type=f32
        ).astype(bf16)
        query[rows] = made[:, :128].reshape(4, 128, 128)
        kv[rows] = made[:, 128:].reshape(4, 128, 256)
        return carry

    lax.fori_loop(0, 4, project_own, 0)

    def project(slot, s, half):
        rows = pl.ds(slot * 16 + 8 * s + 4 * half, 4)
        kv[rows] = (
            jnp.dot(nrm[rows].reshape(512, 512), wqkv[:, 128:], preferred_element_type=f32)
            .astype(bf16)
            .reshape(4, 128, 256)
        )

    def project_slots(s, half, low, high):
        lax.fori_loop(low, high, lambda slot, c: (project(slot, s, half), c)[1], 0)

    def pull(s, j):
        for f in (1, 2):
            z_copy(f, s, j).wait_recv()
        if j < 2:
            x_copy(s, j).start()
        for f in (1, 2):
            if j == 0:
                y_copy(f, s, 0).start()
            a_copy(f, s, j).start()

    def pull_diagonal(s, j):
        x_copy(s, j).wait_recv()
        y_copy(0, s, j).start()
        a_copy(0, s, j).start()

    def pull_near(i):
        n_copy(i).wait_recv()
        m_copy(i).start()

    crossed = ((1, 0), (2, 0), (0, 0), (0, 1))

    def pass_on(s):
        for f, j in crossed:
            y_copy(f, s, j, across).wait_recv()
            b_copy(f, s, j).start()

    def take_direct(s):
        for j in range(3):
            for f in (1, 2):
                a_copy(f, s, j, sib).wait_recv()
        for i in (2 * s, 2 * s + 1):
            m_copy(i, 1 - core).wait_recv()
        project_slots(s, 0, 1, 2)
        project_slots(s, 1, 1, 2)
        project_slots(s, 1, 3, 5)

    def take_rest(s):
        for j in range(2):
            a_copy(0, s, j, sib).wait_recv()
        for f, j in crossed:
            b_copy(f, s, j, corner).wait_recv()
        project_slots(s, 0, 2, 5)
        project_slots(s, 1, 2, 3)

    scale = 1.0 / math.sqrt(128)
    lane_entry = lax.broadcasted_iota(jnp.int32, (1, KMAX * NODE_BLK), 1) // NODE_BLK

    def place_of(b, j):
        block = neigh[b, j]
        away = lax.rem(lax.div(block, 8) - d + doms, doms)
        slot = jnp.where(away == 1, 1 + odd, 0)
        slot = jnp.where(away == doms - 1, 2 - odd, slot)
        slot = jnp.where(away == 2, 3, slot)
        slot = jnp.where(away == doms - 2, 4, slot)
        return slot * 16 + lax.rem(block, 8)

    def attend(b, s):
        places = [place_of(b, j) + s * 8 for j in range(KMAX)]
        keys = jnp.concatenate([kv[place, :, :128] for place in places], axis=0)
        values = jnp.concatenate([kv[place, :, 128:] for place in places], axis=0)
        scores = lax.dot_general(
            query[s * 8 + b], keys, (((1,), (1,)), ((), ())), preferred_element_type=f32
        )
        scores = jnp.where(lane_entry < live[b], scores, -1e30)
        top = jnp.max(scores, axis=1, keepdims=True)
        weights = jnp.exp((scores - top) * scale)
        whole = jnp.sum(weights, axis=1, keepdims=True)
        mixed = jnp.dot(weights.astype(bf16), values, preferred_element_type=f32)
        return (mixed / whole).astype(bf16)

    def attend_pair(owner, s):
        return jnp.concatenate([attend(2 * owner + r, s) for r in range(2)], axis=0)

    def h_copy(k, s, src_tp=t):
        owner = lax.rem(t + 1 + k, 4)
        return remote(
            outgoing.at[3 * s + k], heads.at[src_tp, pl.ds(s * 256, 256)], h_s.at[3 * s + k],
            h_r.at[3 * s + k], d, owner,
        )

    def attend_away(s, low, high):
        def one(k, carry):
            outgoing[3 * s + k] = attend_pair(lax.rem(t + 1 + k, 4), s)
            h_copy(k, s).start()
            return carry

        lax.fori_loop(low, high, one, 0)

    def attend_here(s):
        heads[t, s * 256 : (s + 1) * 256] = attend_pair(t, s)

    def spread(ready):
        for w in ready:
            wy_copy(w, across).wait_recv()
            wx_copy(w).start()
            w0_copy(w).start()

    for j in range(3):
        pull(0, j)
    wy_copy(2).start()
    pull_diagonal(0, 0)
    pull_diagonal(0, 1)
    n_copy(2).start()
    pull_near(0)
    pull_near(1)
    pull(1, 0)
    n_copy(3).start()
    take_direct(0)
    pass_on(0)
    take_rest(0)
    spread((0, 1))
    attend_away(0, 0, 1)
    pull(1, 1)
    attend_away(0, 1, 3)
    pull_diagonal(1, 0)
    spread((2,))
    attend_here(0)
    pull(1, 2)
    pull_diagonal(1, 1)
    pull_near(2)
    pull_near(3)
    take_direct(1)
    pass_on(1)
    take_rest(1)
    attend_away(1, 0, 3)
    for w in range(3):
        wx_copy(w, 1 - odd).wait_recv()
        w1_copy(w).start()
    attend_here(1)
    for k in range(3):
        wa_copy(k, sib).wait_recv()
        w0_copy(k, corner).wait_recv()
        w1_copy(k, corner).wait_recv()

    def o_copy(k, s, owner=t):
        peer = lax.rem(t + 1 + k, 4)
        return remote(
            cols.at[peer, pl.ds(s * 256, 256)],
            out.at[s, pl.ds(pl.multiple_of(owner * 256, 256), 256)],
            o_s.at[k, s], o_r.at[k, s], d, peer,
        )

    def finish(s):
        for k in range(3):
            h_copy(k, s, lax.rem(t + 3 - k, 4)).wait_recv()
        rows = slice(s * 256, (s + 1) * 256)
        attn = jnp.zeros((256, 512), f32)
        for h in range(HEADS):
            attn += (
                jnp.dot(heads[h, rows], wout_all[h], preferred_element_type=f32)
                .astype(bf16)
                .astype(f32)
            )
        after = state[pl.ds(8 * s + 2 * t, 2)].reshape(256, 512).astype(f32) + attn
        normed2[...] = layer_norm(after, gain[1, s : s + 1], shift[1, s : s + 1]).astype(bf16)

        def hidden_group(g, total):
            pre = jnp.dot(normed2[...], wup_all[g], preferred_element_type=f32)
            hidden = (0.5 * pre * (1.0 + jnp.tanh(0.5 * pre))).astype(bf16)
            term = jnp.dot(hidden, wdown_all[g], preferred_element_type=f32)
            return total + term.astype(bf16).astype(f32)

        total = lax.fori_loop(0, 4, hidden_group, after)
        for j in range(4):
            cols[j, rows] = total[:, j * 128 : (j + 1) * 128].astype(bf16)
        for k in range(3):
            o_copy(k, s).start()
        out[s, pl.ds(pl.multiple_of(t * 256, 256), 256)] = cols[t, rows]

    for s in range(2):
        finish(s)

    for s in range(2):
        for j in range(3):
            for f in (1, 2):
                z_copy(f, s, j).wait_send()
                a_copy(f, s, j).wait_send()
        for j in range(2):
            x_copy(s, j).wait_send()
            a_copy(0, s, j).wait_send()
        for f, j in crossed:
            y_copy(f, s, j).wait_send()
            b_copy(f, s, j).wait_send()
    for i in range(4):
        n_copy(i).wait_send()
        m_copy(i).wait_send()
    for k in range(3):
        for copy in (wy_copy, wa_copy, wx_copy, w0_copy, w1_copy):
            copy(k).wait_send()
        for s in range(2):
            h_copy(k, s).wait_send()
    for s in range(2):
        for k in range(3):
            o_copy(k, s, lax.rem(t + 3 - k, 4)).wait_recv()
            o_copy(k, s).wait_send()


def local(
    state, norm_gain, norm_shift, qkv_weight, out_weight, up_weight, down_weight, neighbours, counts
):
    samples, row_count, feat = state.shape
    per_dev = row_count // NODE_BLK
    bf16 = jnp.bfloat16
    dma = pltpu.SemaphoreType.DMA
    smem = pl.BlockSpec(memory_space=pltpu.SMEM)
    vmem = pl.BlockSpec(memory_space=pltpu.VMEM)
    anywhere = pl.BlockSpec(memory_space=pl.ANY)
    pairs = [dma((2,)), dma((4,))]
    for shape in [(2, 6), (3, 4), (3, 6), (3, 4)] + [(4,)] * 3 + [(3,)] * 5 + [(6,), (3, 2)]:
        pairs += [dma(shape), dma(shape)]
    return pl.pallas_call(
        layer_kernel,
        out_shape=jax.ShapeDtypeStruct((samples, row_count, 128), bf16),
        in_specs=[smem, smem, vmem, vmem] + [anywhere] * 5,
        out_specs=vmem,
        scratch_shapes=[
            pltpu.VMEM((16, 128, 512), bf16),
            pltpu.VMEM((3, 512, 128), bf16),
            pltpu.VMEM((512, 384), bf16),
            pltpu.VMEM((80, 128, 512), bf16),
            pltpu.VMEM((80, 128, 256), bf16),
            pltpu.VMEM((16, 128, 128), bf16),
            pltpu.VMEM((4, 512, 128), bf16),
            pltpu.VMEM((6, 256, 128), bf16),
            pltpu.VMEM((4, 128, 512), bf16),
            pltpu.VMEM((4, 512, 512), bf16),
            pltpu.VMEM((4, 512, 512), bf16),
            pltpu.VMEM((256, 512), bf16),
            pltpu.VMEM((4, 512, 128), bf16),
        ]
        + pairs,
        compiler_params=pltpu.CompilerParams(
            collective_id=0, has_side_effects=True, vmem_limit_bytes=62 * 2**20
        ),
    )(
        neighbours,
        counts,
        norm_gain,
        norm_shift,
        state.reshape(samples * per_dev, NODE_BLK, feat),
        jnp.transpose(qkv_weight, (1, 0, 2)),
        out_weight,
        up_weight,
        down_weight,
    )


def solution(mesh):
    placed = (
        P(None, "dom", None),
        P(),
        P(),
        P(None, None, "tp"),
        P("tp", None),
        P(None, "tp"),
        P("tp", None),
        P("dom", None),
        P("dom"),
    )
    return jax.shard_map(
        local, mesh=mesh, in_specs=placed, out_specs=P(None, "dom", "tp"), check_vma=False
    )
```

```python
import math

import jax
import jax.numpy as jnp
from jax import lax
from jax.experimental import pallas as pl
from jax.experimental.pallas import tpu as pltpu
from jax.sharding import PartitionSpec as P

HEADS = 4
NODE_BLK = 128
KMAX = 8


def layer_norm(values, gain_row, shift_row):
    row_mean = jnp.mean(values, axis=-1, keepdims=True)
    centred = values - row_mean
    spread = jnp.mean(centred * centred, axis=-1, keepdims=True)
    return centred * lax.rsqrt(spread + 1e-05) * gain_row + shift_row


def layer_kernel(
    neigh, live, gain, shift, state_in, wqkv_in, wout_in, wup_in, wdown_in, out,
    state, wqkv_raw, wqkv, nrm, kv, query, heads, outgoing, wout_all, wup_all, wdown_all, normed2,
    cols, c_state, c_w,
    z_s, z_r, y_s, y_r, a_s, a_r, b_s, b_r, x_s, x_r, n_s, n_r, m_s, m_r,
    wy_s, wy_r, wa_s, wa_r, wx_s, wx_r, w0_s, w0_r, w1_s, w1_r, h_s, h_r, o_s, o_r,
):
    d = lax.axis_index("dom")
    t = lax.axis_index("tp")
    doms = lax.axis_size("dom")
    odd = lax.rem(d, 2)
    near = d + 1 - 2 * odd
    plus = lax.rem(d + 2, doms)
    minus = lax.rem(d + doms - 2, doms)
    core = lax.rem(t, 2)
    sib = t + 1 - 2 * core
    across = lax.rem(t + 2, 4)
    corner = lax.rem(sib + 2, 4)
    f32 = jnp.float32
    bf16 = jnp.bfloat16

    def remote(src, dst, send, recv, dd, tt):
        return pltpu.make_async_remote_copy(
            src_ref=src, dst_ref=dst, send_sem=send, recv_sem=recv, device_id=(dd, tt),
            device_id_type=pl.DeviceIdType.MESH,
        )

    barrier = pltpu.get_barrier_semaphore()
    for partner in [(near, t), (plus, t), (minus, t), (d, sib), (d, across), (d, corner)]:
        pl.semaphore_signal(
            barrier, inc=1, device_id=partner, device_id_type=pl.DeviceIdType.MESH
        )

    def state_copy(s):
        rows = pl.ds(8 * s, 8)
        return pltpu.make_async_copy(state_in.at[rows], state.at[rows], c_state.at[s])

    shards = ((wout_in, wout_all), (wup_in, wup_all), (wdown_in, wdown_all))
    own_copies = [pltpu.make_async_copy(wqkv_in, wqkv_raw, c_w.at[3])] + [
        pltpu.make_async_copy(shard, full.at[t], c_w.at[k])
        for k, (shard, full) in enumerate(shards)
    ]
    for s in range(2):
        state_copy(s).start()
    for copy in own_copies:
        copy.start()

    def norm_units(s, first, count, around=8):
        def norm_one(i, inner):
            u = 8 * s + lax.rem(first + i, around)
            nrm[u] = layer_norm(
                state[u].astype(f32), gain[0, s : s + 1], shift[0, s : s + 1]
            ).astype(bf16)
            return inner

        lax.fori_loop(0, count, norm_one, 0)

    def unit(rank, j):
        side = lax.div(rank, 2)
        shared = 4 + 2 * lax.rem(rank, 2)
        return (rank, shared + side, shared + 1 - side)[j]

    def z_copy(f, s, j):
        u = 8 * s + unit(t, j)
        return remote(
            nrm.at[u], nrm.at[(2 + f) * 16 + u], z_s.at[f - 1, 3 * s + j],
            z_r.at[f - 1, 3 * s + j], (minus, plus)[f - 1], t,
        )

    def x_copy(s, j):
        u = 8 * s + unit(t, j)
        k = 2 * s + j
        return remote(
            nrm.at[(3 + odd) * 16 + u], nrm.at[2 * 16 + u], x_s.at[k], x_r.at[k], near, t
        )

    def y_copy(f, s, j, owner=t):
        u = (2 + f) * 16 + 8 * s + unit(owner, j)
        k = 2 * s + j
        return remote(nrm.at[u], nrm.at[u], y_s.at[f, k], y_r.at[f, k], d, across)

    def a_copy(f, s, j, owner=t):
        u = (2 + f) * 16 + 8 * s + unit(owner, j)
        k = 3 * s + j
        return remote(nrm.at[u], nrm.at[u], a_s.at[f, k], a_r.at[f, k], d, sib)

    def b_copy(f, s, j, owner=across):
        u = (2 + f) * 16 + 8 * s + unit(owner, j)
        k = 2 * s + j
        return remote(nrm.at[u], nrm.at[u], b_s.at[f, k], b_r.at[f, k], d, sib)

    def n_copy(i):
        u = 8 * (i // 2) + 4 * core + 2 * (i % 2)
        return remote(
            nrm.at[pl.ds(u, 2)], nrm.at[pl.ds(16 + u, 2)], n_s.at[i], n_r.at[i], near, t
        )

    def m_copy(i, side=core):
        u = 16 + 8 * (i // 2) + 4 * side + 2 * (i % 2)
        return remote(nrm.at[pl.ds(u, 2)], nrm.at[pl.ds(u, 2)], m_s.at[i], m_r.at[i], d, sib)

    def part(k, owner, half):
        if k == 2:
            return wdown_all.at[owner]
        rows = shards[k][0].shape[0] // 2
        return shards[k][1].at[owner, pl.ds(pl.multiple_of(half * rows, 64), rows)]

    def wa_copy(k, owner=t):
        full = shards[k][1]
        return remote(full.at[owner], full.at[owner], wa_s.at[k], wa_r.at[k], d, sib)

    def wy_copy(k, owner=t):
        ref = part(k, owner, odd)
        return remote(ref, ref, wy_s.at[k], wy_r.at[k], d, across)

    def wx_copy(k, half=odd):
        ref = part(k, across, half)
        return remote(ref, ref, wx_s.at[k], wx_r.at[k], near, t)

    def w0_copy(k, owner=across):
        ref = part(k, owner, odd)
        return remote(ref, ref, w0_s.at[k], w0_r.at[k], d, sib)

    def w1_copy(k, owner=across):
        ref = part(k, owner, 1 - odd)
        return remote(ref, ref, w1_s.at[k], w1_r.at[k], d, sib)

    state_copy(0).wait()
    norm_units(0, t, 1)
    norm_units(0, 4 + 2 * core, 2)
    pl.semaphore_wait(barrier, 6)
    for j in range(3):
        for f in (1, 2):
            z_copy(f, 0, j).start()
    norm_units(0, t + 1, 3, 4)
    norm_units(0, 6 - 2 * core, 2)
    n_copy(0).start()
    n_copy(1).start()
    for copy in own_copies:
        copy.wait()
    for k in range(2):
        wy_copy(k).start()
    state_copy(1).wait()
    norm_units(1, 0, 8)
    for k in range(3):
        wa_copy(k).start()
    for c in range(3):
        wqkv[:, c * 128 : (c + 1) * 128] = wqkv_raw[c]

    def project_own(k, carry):
        rows = pl.ds(4 * k, 4)
        made = jnp.dot(
            nrm[rows].reshape(512, 512), wqkv[...], preferred_element_type=f32
        ).astype(bf16)
        query[rows] = made[:, :128].reshape(4, 128, 128)
        kv[rows] = made[:, 128:].reshape(4, 128, 256)
        return carry

    lax.fori_loop(0, 4, project_own, 0)

    def project(slot, s, half):
        rows = pl.ds(slot * 16 + 8 * s + 4 * half, 4)
        kv[rows] = (
            jnp.dot(nrm[rows].reshape(512, 512), wqkv[:, 128:], preferred_element_type=f32)
            .astype(bf16)
            .reshape(4, 128, 256)
        )

    def project_slots(s, half, low, high):
        lax.fori_loop(low, high, lambda slot, c: (project(slot, s, half), c)[1], 0)

    def pull(s, j):
        for f in (1, 2):
            z_copy(f, s, j).wait_recv()
            if s == 0:
                z_copy(f, 1, j).start()
        if j < 2:
            x_copy(s, j).start()
        for f in (1, 2):
            if j == 0:
                y_copy(f, s, 0).start()
            a_copy(f, s, j).start()

    def pull_diagonal(s, j):
        x_copy(s, j).wait_recv()
        y_copy(0, s, j).start()
        a_copy(0, s, j).start()

    def pull_near(i):
        n_copy(i).wait_recv()
        m_copy(i).start()

    crossed = ((1, 0), (2, 0), (0, 0), (0, 1))

    def pass_on(s):
        for f, j in crossed:
            y_copy(f, s, j, across).wait_recv()
            b_copy(f, s, j).start()

    def take_direct(s):
        for j in range(3):
            for f in (1, 2):
                a_copy(f, s, j, sib).wait_recv()
        for i in (2 * s, 2 * s + 1):
            m_copy(i, 1 - core).wait_recv()
        project_slots(s, 0, 1, 2)
        project_slots(s, 1, 1, 2)
        project_slots(s, 1, 3, 5)

    def take_rest(s):
        for j in range(2):
            a_copy(0, s, j, sib).wait_recv()
        for f, j in crossed:
            b_copy(f, s, j, corner).wait_recv()
        project_slots(s, 0, 2, 5)
        project_slots(s, 1, 2, 3)

    scale = 1.0 / math.sqrt(128)
    lane_entry = lax.broadcasted_iota(jnp.int32, (1, KMAX * NODE_BLK), 1) // NODE_BLK

    def place_of(b, j):
        block = neigh[b, j]
        away = lax.rem(lax.div(block, 8) - d + doms, doms)
        slot = jnp.where(away == 1, 1 + odd, 0)
        slot = jnp.where(away == doms - 1, 2 - odd, slot)
        slot = jnp.where(away == 2, 3, slot)
        slot = jnp.where(away == doms - 2, 4, slot)
        return slot * 16 + lax.rem(block, 8)

    def attend(b, s):
        places = [place_of(b, j) + s * 8 for j in range(KMAX)]
        keys = jnp.concatenate([kv[place, :, :128] for place in places], axis=0)
        values = jnp.concatenate([kv[place, :, 128:] for place in places], axis=0)
        scores = lax.dot_general(
            query[s * 8 + b], keys, (((1,), (1,)), ((), ())), preferred_element_type=f32
        )
        scores = jnp.where(lane_entry < live[b], scores, -1e30)
        top = jnp.max(scores, axis=1, keepdims=True)
        weights = jnp.exp((scores - top) * scale)
        whole = jnp.sum(weights, axis=1, keepdims=True)
        mixed = jnp.dot(weights.astype(bf16), values, preferred_element_type=f32)
        return (mixed / whole).astype(bf16)

    def attend_pair(owner, s):
        return jnp.concatenate([attend(2 * owner + r, s) for r in range(2)], axis=0)

    def h_copy(k, s, src_tp=t):
        owner = lax.rem(t + 1 + k, 4)
        return remote(
            outgoing.at[3 * s + k], heads.at[src_tp, pl.ds(s * 256, 256)], h_s.at[3 * s + k],
            h_r.at[3 * s + k], d, owner,
        )

    def attend_away(s, low, high):
        def one(k, carry):
            outgoing[3 * s + k] = attend_pair(lax.rem(t + 1 + k, 4), s)
            h_copy(k, s).start()
            return carry

        lax.fori_loop(low, high, one, 0)

    def attend_here(s):
        heads[t, s * 256 : (s + 1) * 256] = attend_pair(t, s)

    def spread(ready):
        for w in ready:
            wy_copy(w, across).wait_recv()
            wx_copy(w).start()
            w0_copy(w).start()

    for j in range(3):
        pull(0, j)
    pull_diagonal(0, 0)
    pull_diagonal(0, 1)
    n_copy(2).start()
    pull_near(0)
    pull_near(1)
    take_direct(0)
    pass_on(0)
    pull(1, 0)
    n_copy(3).start()
    take_rest(0)
    attend_away(0, 0, 1)
    pull(1, 1)
    attend_away(0, 1, 2)
    pull_diagonal(1, 0)
    attend_away(0, 2, 3)
    pull(1, 2)
    pull_diagonal(1, 1)
    wy_copy(2).start()
    spread((0, 1))
    pull_near(2)
    pull_near(3)
    attend_here(0)
    take_direct(1)
    pass_on(1)
    take_rest(1)
    attend_away(1, 0, 3)
    for w in range(2):
        wx_copy(w, 1 - odd).wait_recv()
        w1_copy(w).start()
    wy_copy(2, across).wait_recv()
    w0_copy(2).start()
    attend_here(1)
    for k in range(3):
        wa_copy(k, sib).wait_recv()
        w0_copy(k, corner).wait_recv()
    for k in range(2):
        w1_copy(k, corner).wait_recv()

    def o_copy(k, s, owner=t):
        peer = lax.rem(t + 1 + k, 4)
        return remote(
            cols.at[peer, pl.ds(s * 256, 256)],
            out.at[s, pl.ds(pl.multiple_of(owner * 256, 256), 256)],
            o_s.at[k, s], o_r.at[k, s], d, peer,
        )

    def finish(s):
        for k in range(3):
            h_copy(k, s, lax.rem(t + 3 - k, 4)).wait_recv()
        rows = slice(s * 256, (s + 1) * 256)
        attn = jnp.zeros((256, 512), f32)
        for h in range(HEADS):
            attn += (
                jnp.dot(heads[h, rows], wout_all[h], preferred_element_type=f32)
                .astype(bf16)
                .astype(f32)
            )
        after = state[pl.ds(8 * s + 2 * t, 2)].reshape(256, 512).astype(f32) + attn
        normed2[...] = layer_norm(after, gain[1, s : s + 1], shift[1, s : s + 1]).astype(bf16)

        def hidden_group(g, total):
            pre = jnp.dot(normed2[...], wup_all[g], preferred_element_type=f32)
            hidden = (0.5 * pre * (1.0 + jnp.tanh(0.5 * pre))).astype(bf16)
            term = jnp.dot(hidden, wdown_all[g], preferred_element_type=f32)
            return total + term.astype(bf16).astype(f32)

        total = lax.fori_loop(0, 4, hidden_group, after)
        for j in range(4):
            cols[j, rows] = total[:, j * 128 : (j + 1) * 128].astype(bf16)
        for k in range(3):
            o_copy(k, s).start()
        out[s, pl.ds(pl.multiple_of(t * 256, 256), 256)] = cols[t, rows]

    for s in range(2):
        finish(s)

    for s in range(2):
        for j in range(3):
            for f in (1, 2):
                z_copy(f, s, j).wait_send()
                a_copy(f, s, j).wait_send()
        for j in range(2):
            x_copy(s, j).wait_send()
            a_copy(0, s, j).wait_send()
        for f, j in crossed:
            y_copy(f, s, j).wait_send()
            b_copy(f, s, j).wait_send()
    for i in range(4):
        n_copy(i).wait_send()
        m_copy(i).wait_send()
    for k in range(3):
        for copy in (wy_copy, wa_copy, w0_copy) + ((wx_copy, w1_copy) if k < 2 else ()):
            copy(k).wait_send()
        for s in range(2):
            h_copy(k, s).wait_send()
    for s in range(2):
        for k in range(3):
            o_copy(k, s, lax.rem(t + 3 - k, 4)).wait_recv()
            o_copy(k, s).wait_send()


def local(
    state, norm_gain, norm_shift, qkv_weight, out_weight, up_weight, down_weight, neighbours, counts
):
    samples, row_count, feat = state.shape
    per_dev = row_count // NODE_BLK
    bf16 = jnp.bfloat16
    dma = pltpu.SemaphoreType.DMA
    smem = pl.BlockSpec(memory_space=pltpu.SMEM)
    vmem = pl.BlockSpec(memory_space=pltpu.VMEM)
    anywhere = pl.BlockSpec(memory_space=pl.ANY)
    pairs = [dma((2,)), dma((4,))]
    for shape in [(2, 6), (3, 4), (3, 6), (3, 4)] + [(4,)] * 3 + [(3,)] * 5 + [(6,), (3, 2)]:
        pairs += [dma(shape), dma(shape)]
    return pl.pallas_call(
        layer_kernel,
        out_shape=jax.ShapeDtypeStruct((samples, row_count, 128), bf16),
        in_specs=[smem, smem, vmem, vmem] + [anywhere] * 5,
        out_specs=vmem,
        scratch_shapes=[
            pltpu.VMEM((16, 128, 512), bf16),
            pltpu.VMEM((3, 512, 128), bf16),
            pltpu.VMEM((512, 384), bf16),
            pltpu.VMEM((80, 128, 512), bf16),
            pltpu.VMEM((80, 128, 256), bf16),
            pltpu.VMEM((16, 128, 128), bf16),
            pltpu.VMEM((4, 512, 128), bf16),
            pltpu.VMEM((6, 256, 128), bf16),
            pltpu.VMEM((4, 128, 512), bf16),
            pltpu.VMEM((4, 512, 512), bf16),
            pltpu.VMEM((4, 512, 512), bf16),
            pltpu.VMEM((256, 512), bf16),
            pltpu.VMEM((4, 512, 128), bf16),
        ]
        + pairs,
        compiler_params=pltpu.CompilerParams(
            collective_id=0, has_side_effects=True, vmem_limit_bytes=62 * 2**20
        ),
    )(
        neighbours,
        counts,
        norm_gain,
        norm_shift,
        state.reshape(samples * per_dev, NODE_BLK, feat),
        jnp.transpose(qkv_weight, (1, 0, 2)),
        out_weight,
        up_weight,
        down_weight,
    )


def solution(mesh):
    placed = (
        P(None, "dom", None),
        P(),
        P(),
        P(None, None, "tp"),
        P("tp", None),
        P(None, "tp"),
        P("tp", None),
        P("dom", None),
        P("dom"),
    )
    return jax.shard_map(
        local, mesh=mesh, in_specs=placed, out_specs=P(None, "dom", "tp"), check_vma=False
    )
```

```python
import math

import jax
import jax.numpy as jnp
from jax import lax
from jax.experimental import pallas as pl
from jax.experimental.pallas import tpu as pltpu
from jax.sharding import PartitionSpec as P

HEADS = 4
NODE_BLK = 128
KMAX = 8


def layer_norm(values, gain_row, shift_row):
    row_mean = jnp.mean(values, axis=-1, keepdims=True)
    centred = values - row_mean
    spread = jnp.mean(centred * centred, axis=-1, keepdims=True)
    return centred * lax.rsqrt(spread + 1e-05) * gain_row + shift_row


def layer_kernel(
    neigh, live, gain, shift, state_in, wqkv_in, wout_in, wup_in, wdown_in, out,
    state, wqkv_raw, wqkv, nrm, kv, query, heads, outgoing, wout_all, wup_all, wdown_all, normed2,
    cols, c_state, c_w,
    z_s, z_r, y_s, y_r, a_s, a_r, b_s, b_r, x_s, x_r, n_s, n_r, m_s, m_r,
    wy_s, wy_r, wa_s, wa_r, wx_s, wx_r, w0_s, w0_r, w1_s, w1_r, h_s, h_r, o_s, o_r,
):
    d = lax.axis_index("dom")
    t = lax.axis_index("tp")
    doms = lax.axis_size("dom")
    odd = lax.rem(d, 2)
    near = d + 1 - 2 * odd
    plus = lax.rem(d + 2, doms)
    minus = lax.rem(d + doms - 2, doms)
    core = lax.rem(t, 2)
    sib = t + 1 - 2 * core
    across = lax.rem(t + 2, 4)
    corner = lax.rem(sib + 2, 4)
    f32 = jnp.float32
    bf16 = jnp.bfloat16

    def remote(src, dst, send, recv, dd, tt):
        return pltpu.make_async_remote_copy(
            src_ref=src, dst_ref=dst, send_sem=send, recv_sem=recv, device_id=(dd, tt),
            device_id_type=pl.DeviceIdType.MESH,
        )

    barrier = pltpu.get_barrier_semaphore()
    for partner in [(near, t), (plus, t), (minus, t), (d, sib), (d, across), (d, corner)]:
        pl.semaphore_signal(
            barrier, inc=1, device_id=partner, device_id_type=pl.DeviceIdType.MESH
        )

    def state_copy(s):
        rows = pl.ds(8 * s, 8)
        return pltpu.make_async_copy(state_in.at[rows], state.at[rows], c_state.at[s])

    shards = ((wout_in, wout_all), (wup_in, wup_all), (wdown_in, wdown_all))
    own_copies = [pltpu.make_async_copy(wqkv_in, wqkv_raw, c_w.at[3])] + [
        pltpu.make_async_copy(shard, full.at[t], c_w.at[k])
        for k, (shard, full) in enumerate(shards)
    ]
    for s in range(2):
        state_copy(s).start()
    for copy in own_copies:
        copy.start()

    def norm_units(s, first, count, around=8):
        def norm_one(i, inner):
            u = 8 * s + lax.rem(first + i, around)
            nrm[u] = layer_norm(
                state[u].astype(f32), gain[0, s : s + 1], shift[0, s : s + 1]
            ).astype(bf16)
            return inner

        lax.fori_loop(0, count, norm_one, 0)

    def unit(rank, j):
        side = lax.div(rank, 2)
        shared = 4 + 2 * lax.rem(rank, 2)
        return (rank, shared + side, shared + 1 - side)[j]

    def z_copy(f, s, j):
        u = 8 * s + unit(t, j)
        return remote(
            nrm.at[u], nrm.at[(2 + f) * 16 + u], z_s.at[f - 1, 3 * s + j],
            z_r.at[f - 1, 3 * s + j], (minus, plus)[f - 1], t,
        )

    def x_copy(s, j):
        u = 8 * s + unit(t, j)
        k = 2 * s + j
        return remote(
            nrm.at[(3 + odd) * 16 + u], nrm.at[2 * 16 + u], x_s.at[k], x_r.at[k], near, t
        )

    def y_copy(f, s, j, owner=t):
        u = (2 + f) * 16 + 8 * s + unit(owner, j)
        k = 2 * s + j
        return remote(nrm.at[u], nrm.at[u], y_s.at[f, k], y_r.at[f, k], d, across)

    def a_copy(f, s, j, owner=t):
        u = (2 + f) * 16 + 8 * s + unit(owner, j)
        k = 3 * s + j
        return remote(nrm.at[u], nrm.at[u], a_s.at[f, k], a_r.at[f, k], d, sib)

    def b_copy(f, s, j, owner=across):
        u = (2 + f) * 16 + 8 * s + unit(owner, j)
        k = 2 * s + j
        return remote(nrm.at[u], nrm.at[u], b_s.at[f, k], b_r.at[f, k], d, sib)

    def n_copy(i):
        u = 8 * (i // 2) + 4 * core + 2 * (i % 2)
        return remote(
            nrm.at[pl.ds(u, 2)], nrm.at[pl.ds(16 + u, 2)], n_s.at[i], n_r.at[i], near, t
        )

    def m_copy(i, side=core):
        u = 16 + 8 * (i // 2) + 4 * side + 2 * (i % 2)
        return remote(nrm.at[pl.ds(u, 2)], nrm.at[pl.ds(u, 2)], m_s.at[i], m_r.at[i], d, sib)

    def part(k, owner, half):
        if k == 2:
            return wdown_all.at[owner]
        rows = shards[k][0].shape[0] // 2
        return shards[k][1].at[owner, pl.ds(pl.multiple_of(half * rows, 64), rows)]

    def wa_copy(k, owner=t):
        full = shards[k][1]
        return remote(full.at[owner], full.at[owner], wa_s.at[k], wa_r.at[k], d, sib)

    def wy_copy(k, owner=t):
        ref = part(k, owner, odd)
        return remote(ref, ref, wy_s.at[k], wy_r.at[k], d, across)

    def wx_copy(k, half=odd):
        ref = part(k, across, half)
        return remote(ref, ref, wx_s.at[k], wx_r.at[k], near, t)

    def w0_copy(k, owner=across):
        ref = part(k, owner, odd)
        return remote(ref, ref, w0_s.at[k], w0_r.at[k], d, sib)

    def w1_copy(k, owner=across):
        ref = part(k, owner, 1 - odd)
        return remote(ref, ref, w1_s.at[k], w1_r.at[k], d, sib)

    state_copy(0).wait()
    norm_units(0, t, 1)
    norm_units(0, 4 + 2 * core, 2)
    pl.semaphore_wait(barrier, 6)
    for j in range(3):
        for f in (1, 2):
            z_copy(f, 0, j).start()
    norm_units(0, t + 1, 3, 4)
    norm_units(0, 6 - 2 * core, 2)
    n_copy(0).start()
    n_copy(1).start()
    for copy in own_copies:
        copy.wait()
    for k in range(2):
        wy_copy(k).start()
    state_copy(1).wait()
    norm_units(1, 0, 8)
    for k in range(3):
        wa_copy(k).start()
    for c in range(3):
        wqkv[:, c * 128 : (c + 1) * 128] = wqkv_raw[c]

    def project_own(k, carry):
        rows = pl.ds(4 * k, 4)
        made = jnp.dot(
            nrm[rows].reshape(512, 512), wqkv[...], preferred_element_type=f32
        ).astype(bf16)
        query[rows] = made[:, :128].reshape(4, 128, 128)
        kv[rows] = made[:, 128:].reshape(4, 128, 256)
        return carry


    def project(slot, s, half):
        rows = pl.ds(slot * 16 + 8 * s + 4 * half, 4)
        kv[rows] = (
            jnp.dot(nrm[rows].reshape(512, 512), wqkv[:, 128:], preferred_element_type=f32)
            .astype(bf16)
            .reshape(4, 128, 256)
        )

    def project_slots(s, half, low, high):
        lax.fori_loop(low, high, lambda slot, c: (project(slot, s, half), c)[1], 0)

    def pull(s, j):
        for f in (1, 2):
            z_copy(f, s, j).wait_recv()
            if s == 0:
                z_copy(f, 1, j).start()
        if j < 2:
            x_copy(s, j).start()
        for f in (1, 2):
            if j == 0:
                y_copy(f, s, 0).start()
            a_copy(f, s, j).start()

    def pull_diagonal(s, j):
        x_copy(s, j).wait_recv()
        y_copy(0, s, j).start()
        a_copy(0, s, j).start()

    def pull_near(i):
        n_copy(i).wait_recv()
        m_copy(i).start()

    crossed = ((1, 0), (2, 0), (0, 0), (0, 1))

    def pass_on(s):
        for f, j in crossed:
            y_copy(f, s, j, across).wait_recv()
            b_copy(f, s, j).start()

    def take_direct(s):
        for j in range(3):
            for f in (1, 2):
                a_copy(f, s, j, sib).wait_recv()
        for i in (2 * s, 2 * s + 1):
            m_copy(i, 1 - core).wait_recv()
        project_slots(s, 0, 1, 2)
        project_slots(s, 1, 1, 2)
        project_slots(s, 1, 3, 5)

    def take_rest(s):
        for j in range(2):
            a_copy(0, s, j, sib).wait_recv()
        for f, j in crossed:
            b_copy(f, s, j, corner).wait_recv()
        project_slots(s, 0, 2, 5)
        project_slots(s, 1, 2, 3)

    scale = math.log2(math.e) / math.sqrt(128)
    lane_entry = lax.broadcasted_iota(jnp.int32, (1, KMAX * NODE_BLK), 1) // NODE_BLK

    def place_of(b, j):
        block = neigh[b, j]
        away = lax.rem(lax.div(block, 8) - d + doms, doms)
        slot = jnp.where(away == 1, 1 + odd, 0)
        slot = jnp.where(away == doms - 1, 2 - odd, slot)
        slot = jnp.where(away == 2, 3, slot)
        slot = jnp.where(away == doms - 2, 4, slot)
        return slot * 16 + lax.rem(block, 8)

    def attend(b, s):
        places = [place_of(b, j) + s * 8 for j in range(KMAX)]
        keys = jnp.concatenate([kv[place, :, :128] for place in places], axis=0)
        values = jnp.concatenate([kv[place, :, 128:] for place in places], axis=0)
        values = jnp.concatenate([values, jnp.ones_like(values)], axis=1)
        scores = lax.dot_general(
            query[s * 8 + b], keys, (((1,), (1,)), ((), ())), preferred_element_type=f32
        )
        scores = jnp.where(lane_entry < live[b], scores, -1e30)
        top = jnp.max(scores, axis=1, keepdims=True)
        weights = jnp.exp2((scores - top) * scale).astype(bf16)
        mixed = jnp.dot(weights, values, preferred_element_type=f32)
        return (mixed[:, :128] / mixed[:, 128:]).astype(bf16)

    def attend_pair(owner, s):
        return jnp.concatenate([attend(2 * owner + r, s) for r in range(2)], axis=0)

    def h_copy(k, s, src_tp=t):
        owner = lax.rem(t + 1 + k, 4)
        return remote(
            outgoing.at[3 * s + k], heads.at[src_tp, pl.ds(s * 256, 256)], h_s.at[3 * s + k],
            h_r.at[3 * s + k], d, owner,
        )

    def attend_away(s, low, high):
        def one(k, carry):
            outgoing[3 * s + k] = attend_pair(lax.rem(t + 1 + k, 4), s)
            h_copy(k, s).start()
            return carry

        lax.fori_loop(low, high, one, 0)

    def attend_here(s):
        heads[t, s * 256 : (s + 1) * 256] = attend_pair(t, s)

    def spread(ready):
        for w in ready:
            wy_copy(w, across).wait_recv()
            wx_copy(w).start()
            w0_copy(w).start()

    for j in range(3):
        pull(0, j)
        if j == 1:
            lax.fori_loop(0, 4, project_own, 0)
    pull_diagonal(0, 0)
    pull_diagonal(0, 1)
    n_copy(2).start()
    pull_near(0)
    pull_near(1)
    take_direct(0)
    pass_on(0)
    pull(1, 0)
    n_copy(3).start()
    take_rest(0)
    attend_away(0, 0, 1)
    pull(1, 1)
    attend_away(0, 1, 2)
    pull_diagonal(1, 0)
    attend_away(0, 2, 3)
    pull(1, 2)
    pull_diagonal(1, 1)
    wy_copy(2).start()
    spread((0, 1))
    pull_near(2)
    pull_near(3)
    attend_here(0)
    take_direct(1)
    pass_on(1)
    take_rest(1)
    attend_away(1, 0, 3)
    for w in range(2):
        wx_copy(w, 1 - odd).wait_recv()
        w1_copy(w).start()
    wy_copy(2, across).wait_recv()
    w0_copy(2).start()
    attend_here(1)
    for k in range(3):
        wa_copy(k, sib).wait_recv()
        w0_copy(k, corner).wait_recv()
    for k in range(2):
        w1_copy(k, corner).wait_recv()

    def o_copy(k, s, owner=t):
        peer = lax.rem(t + 1 + k, 4)
        return remote(
            cols.at[peer, pl.ds(s * 256, 256)],
            out.at[s, pl.ds(pl.multiple_of(owner * 256, 256), 256)],
            o_s.at[k, s], o_r.at[k, s], d, peer,
        )

    def finish(s):
        for k in range(3):
            h_copy(k, s, lax.rem(t + 3 - k, 4)).wait_recv()
        rows = slice(s * 256, (s + 1) * 256)
        attn = jnp.zeros((256, 512), f32)
        for h in range(HEADS):
            attn += (
                jnp.dot(heads[h, rows], wout_all[h], preferred_element_type=f32)
                .astype(bf16)
                .astype(f32)
            )
        after = state[pl.ds(8 * s + 2 * t, 2)].reshape(256, 512).astype(f32) + attn
        normed2[...] = layer_norm(after, gain[1, s : s + 1], shift[1, s : s + 1]).astype(bf16)

        def hidden_group(g, total):
            pre = jnp.dot(normed2[...], wup_all[g], preferred_element_type=f32)
            hidden = (0.5 * pre * (1.0 + jnp.tanh(0.5 * pre))).astype(bf16)
            term = jnp.dot(hidden, wdown_all[g], preferred_element_type=f32)
            return total + term.astype(bf16).astype(f32)

        total = lax.fori_loop(0, 4, hidden_group, after, unroll=True)
        for j in range(4):
            cols[j, rows] = total[:, j * 128 : (j + 1) * 128].astype(bf16)
        for k in range(3):
            o_copy(k, s).start()
        out[s, pl.ds(pl.multiple_of(t * 256, 256), 256)] = cols[t, rows]

    for s in range(2):
        finish(s)

    for s in range(2):
        for j in range(3):
            for f in (1, 2):
                z_copy(f, s, j).wait_send()
                a_copy(f, s, j).wait_send()
        for j in range(2):
            x_copy(s, j).wait_send()
            a_copy(0, s, j).wait_send()
        for f, j in crossed:
            y_copy(f, s, j).wait_send()
            b_copy(f, s, j).wait_send()
    for i in range(4):
        n_copy(i).wait_send()
        m_copy(i).wait_send()
    for k in range(3):
        for copy in (wy_copy, wa_copy, w0_copy) + ((wx_copy, w1_copy) if k < 2 else ()):
            copy(k).wait_send()
        for s in range(2):
            h_copy(k, s).wait_send()
    for s in range(2):
        for k in range(3):
            o_copy(k, s, lax.rem(t + 3 - k, 4)).wait_recv()
            o_copy(k, s).wait_send()


def local(
    state, norm_gain, norm_shift, qkv_weight, out_weight, up_weight, down_weight, neighbours, counts
):
    samples, row_count, feat = state.shape
    per_dev = row_count // NODE_BLK
    bf16 = jnp.bfloat16
    dma = pltpu.SemaphoreType.DMA
    smem = pl.BlockSpec(memory_space=pltpu.SMEM)
    vmem = pl.BlockSpec(memory_space=pltpu.VMEM)
    anywhere = pl.BlockSpec(memory_space=pl.ANY)
    pairs = [dma((2,)), dma((4,))]
    for shape in [(2, 6), (3, 4), (3, 6), (3, 4)] + [(4,)] * 3 + [(3,)] * 5 + [(6,), (3, 2)]:
        pairs += [dma(shape), dma(shape)]
    return pl.pallas_call(
        layer_kernel,
        out_shape=jax.ShapeDtypeStruct((samples, row_count, 128), bf16),
        in_specs=[smem, smem, vmem, vmem] + [anywhere] * 5,
        out_specs=vmem,
        scratch_shapes=[
            pltpu.VMEM((16, 128, 512), bf16),
            pltpu.VMEM((3, 512, 128), bf16),
            pltpu.VMEM((512, 384), bf16),
            pltpu.VMEM((80, 128, 512), bf16),
            pltpu.VMEM((80, 128, 256), bf16),
            pltpu.VMEM((16, 128, 128), bf16),
            pltpu.VMEM((4, 512, 128), bf16),
            pltpu.VMEM((6, 256, 128), bf16),
            pltpu.VMEM((4, 128, 512), bf16),
            pltpu.VMEM((4, 512, 512), bf16),
            pltpu.VMEM((4, 512, 512), bf16),
            pltpu.VMEM((256, 512), bf16),
            pltpu.VMEM((4, 512, 128), bf16),
        ]
        + pairs,
        compiler_params=pltpu.CompilerParams(
            collective_id=0, has_side_effects=True, vmem_limit_bytes=62 * 2**20
        ),
    )(
        neighbours,
        counts,
        norm_gain,
        norm_shift,
        state.reshape(samples * per_dev, NODE_BLK, feat),
        jnp.transpose(qkv_weight, (1, 0, 2)),
        out_weight,
        up_weight,
        down_weight,
    )


def solution(mesh):
    placed = (
        P(None, "dom", None),
        P(),
        P(),
        P(None, None, "tp"),
        P("tp", None),
        P(None, "tp"),
        P("tp", None),
        P("dom", None),
        P("dom"),
    )
    return jax.shard_map(
        local, mesh=mesh, in_specs=placed, out_specs=P(None, "dom", "tp"), check_vma=False
    )
```

```python
import math

import jax
import jax.numpy as jnp
from jax import lax
from jax.experimental import pallas as pl
from jax.experimental.pallas import tpu as pltpu
from jax.sharding import PartitionSpec as P

HEADS = 4
NODE_BLK = 128
KMAX = 8
SLOTS = (2, 3, 4, 1)


def layer_norm(values, gain_row, shift_row):
    row_mean = jnp.mean(values, axis=-1, keepdims=True)
    centred = values - row_mean
    spread = jnp.mean(centred * centred, axis=-1, keepdims=True)
    return centred * lax.rsqrt(spread + 1e-05) * gain_row + shift_row


def layer_kernel(
    neigh, live, gain, shift, state_in, wqkv_in, wout_in, wup_in, wdown_in, out,
    state, wqkv_raw, wqkv, nrm, kv, query, heads, outgoing, wout_all, wup_all, wdown_all, normed2,
    cols, c_state, c_w,
    z_s, z_r, y_s, y_r, a_s, a_r, b_s, b_r, x_s, x_r, n_s, n_r,
    wy_s, wy_r, wa_s, wa_r, wx_s, wx_r, w0_s, w0_r, w1_s, w1_r, h_s, h_r, o_s, o_r,
):
    d = lax.axis_index("dom")
    t = lax.axis_index("tp")
    doms = lax.axis_size("dom")
    odd = lax.rem(d, 2)
    near = d + 1 - 2 * odd
    plus = lax.rem(d + 2, doms)
    minus = lax.rem(d + doms - 2, doms)
    core = lax.rem(t, 2)
    sib = t + 1 - 2 * core
    across = lax.rem(t + 2, 4)
    corner = lax.rem(sib + 2, 4)
    f32 = jnp.float32
    bf16 = jnp.bfloat16

    def remote(src, dst, send, recv, dd, tt):
        return pltpu.make_async_remote_copy(
            src_ref=src, dst_ref=dst, send_sem=send, recv_sem=recv, device_id=(dd, tt),
            device_id_type=pl.DeviceIdType.MESH,
        )

    barrier = pltpu.get_barrier_semaphore()
    for partner in [(near, t), (plus, t), (minus, t), (d, sib), (d, across), (d, corner)]:
        pl.semaphore_signal(
            barrier, inc=1, device_id=partner, device_id_type=pl.DeviceIdType.MESH
        )

    def state_copy(s):
        rows = pl.ds(8 * s, 8)
        return pltpu.make_async_copy(state_in.at[rows], state.at[rows], c_state.at[s])

    shards = ((wout_in, wout_all), (wup_in, wup_all), (wdown_in, wdown_all))
    own_copies = [pltpu.make_async_copy(wqkv_in, wqkv_raw, c_w.at[3])] + [
        pltpu.make_async_copy(shard, full.at[t], c_w.at[k])
        for k, (shard, full) in enumerate(shards)
    ]
    for s in range(2):
        state_copy(s).start()
    for copy in own_copies:
        copy.start()

    def norm_units(s, first, count, around=8):
        def norm_one(i, inner):
            u = 8 * s + lax.rem(first + i, around)
            nrm[u] = layer_norm(
                state[u].astype(f32), gain[0, s : s + 1], shift[0, s : s + 1]
            ).astype(bf16)
            return inner

        lax.fori_loop(0, count, norm_one, 0)

    def unit(rank, j):
        side = lax.div(rank, 2)
        shared = 4 + 2 * lax.rem(rank, 2)
        return (rank, shared + side, shared + 1 - side)[j]

    def z_copy(f, s, j):
        u = 8 * s + unit(t, j)
        return remote(
            nrm.at[u], nrm.at[(2 + f) * 16 + u], z_s.at[f - 1, 3 * s + j],
            z_r.at[f - 1, 3 * s + j], (minus, plus)[f - 1], t,
        )

    def x_copy(s, j):
        u = 8 * s + unit(t, j)
        k = 2 * s + j
        return remote(
            nrm.at[(3 + odd) * 16 + u], nrm.at[2 * 16 + u], x_s.at[k], x_r.at[k], near, t
        )

    def y_copy(f, s, j, owner=t):
        u = SLOTS[f] * 16 + 8 * s + unit(owner, j)
        k = 2 * s + j
        return remote(nrm.at[u], nrm.at[u], y_s.at[f, k], y_r.at[f, k], d, across)

    def a_copy(f, s, j, owner=t):
        u = SLOTS[f] * 16 + 8 * s + unit(owner, j)
        k = 3 * s + j
        return remote(nrm.at[u], nrm.at[u], a_s.at[f, k], a_r.at[f, k], d, sib)

    def b_copy(f, s, j, owner=across):
        u = SLOTS[f] * 16 + 8 * s + unit(owner, j)
        k = 2 * s + j
        return remote(nrm.at[u], nrm.at[u], b_s.at[f, k], b_r.at[f, k], d, sib)

    def n_copy(s, j):
        u = 8 * s + unit(t, j)
        k = 3 * s + j
        return remote(nrm.at[u], nrm.at[16 + u], n_s.at[k], n_r.at[k], near, t)

    def part(k, owner, half):
        if k == 2:
            return wdown_all.at[owner]
        rows = shards[k][0].shape[0] // 2
        return shards[k][1].at[owner, pl.ds(pl.multiple_of(half * rows, 64), rows)]

    def wa_copy(k, owner=t):
        full = shards[k][1]
        return remote(full.at[owner], full.at[owner], wa_s.at[k], wa_r.at[k], d, sib)

    def wy_copy(k, owner=t):
        ref = part(k, owner, odd)
        return remote(ref, ref, wy_s.at[k], wy_r.at[k], d, across)

    def wx_copy(k, half=odd):
        ref = part(k, across, half)
        return remote(ref, ref, wx_s.at[k], wx_r.at[k], near, t)

    def w0_copy(k, owner=across):
        ref = part(k, owner, odd)
        return remote(ref, ref, w0_s.at[k], w0_r.at[k], d, sib)

    def w1_copy(k, owner=across):
        ref = part(k, owner, 1 - odd)
        return remote(ref, ref, w1_s.at[k], w1_r.at[k], d, sib)

    state_copy(0).wait()
    norm_units(0, t, 1)
    norm_units(0, 4 + 2 * core, 2)
    pl.semaphore_wait(barrier, 6)
    for j in range(3):
        for f in (1, 2):
            z_copy(f, 0, j).start()
    norm_units(0, t + 1, 3, 4)
    norm_units(0, 6 - 2 * core, 2)
    for j in range(3):
        n_copy(0, j).start()
    for copy in own_copies:
        copy.wait()
    for k in range(2):
        wy_copy(k).start()
    state_copy(1).wait()
    norm_units(1, 0, 8)
    for k in range(3):
        wa_copy(k).start()
    for c in range(3):
        wqkv[:, c * 128 : (c + 1) * 128] = wqkv_raw[c]

    def project_own(k, carry):
        rows = pl.ds(4 * k, 4)
        made = jnp.dot(
            nrm[rows].reshape(512, 512), wqkv[...], preferred_element_type=f32
        ).astype(bf16)
        query[rows] = made[:, :128].reshape(4, 128, 128)
        kv[rows] = made[:, 128:].reshape(4, 128, 256)
        return carry


    def project(slot, s, half):
        rows = pl.ds(slot * 16 + 8 * s + 4 * half, 4)
        kv[rows] = (
            jnp.dot(nrm[rows].reshape(512, 512), wqkv[:, 128:], preferred_element_type=f32)
            .astype(bf16)
            .reshape(4, 128, 256)
        )

    def project_slots(s, half, low, high):
        lax.fori_loop(low, high, lambda slot, c: (project(slot, s, half), c)[1], 0)

    def pull(s, j):
        for f in (1, 2):
            z_copy(f, s, j).wait_recv()
            if s == 0:
                z_copy(f, 1, j).start()
        if j < 2:
            x_copy(s, j).start()
        for f in (1, 2):
            if j == 0:
                y_copy(f, s, 0).start()
            a_copy(f, s, j).start()

    def pull_diagonal(s, j):
        x_copy(s, j).wait_recv()
        y_copy(0, s, j).start()
        a_copy(0, s, j).start()

    def pull_near(s, j):
        n_copy(s, j).wait_recv()
        if s == 0:
            n_copy(1, j).start()
        if j == 0:
            y_copy(3, s, 0).start()
        a_copy(3, s, j).start()

    crossed = ((1, 0), (2, 0), (3, 0), (0, 0), (0, 1))

    def pass_on(s):
        for f, j in crossed:
            y_copy(f, s, j, across).wait_recv()
            b_copy(f, s, j).start()

    def take_direct(s):
        for j in range(3):
            for f in (1, 2, 3):
                a_copy(f, s, j, sib).wait_recv()
        project_slots(s, 1, 1, 2)
        project_slots(s, 1, 3, 5)

    def take_rest(s):
        for j in range(2):
            a_copy(0, s, j, sib).wait_recv()
        for f, j in crossed:
            b_copy(f, s, j, corner).wait_recv()
        project_slots(s, 0, 1, 5)
        project_slots(s, 1, 2, 3)

    scale = math.log2(math.e) / math.sqrt(128)
    lane_entry = lax.broadcasted_iota(jnp.int32, (1, KMAX * NODE_BLK), 1) // NODE_BLK

    def place_of(b, j):
        block = neigh[b, j]
        away = lax.rem(lax.div(block, 8) - d + doms, doms)
        slot = jnp.where(away == 1, 1 + odd, 0)
        slot = jnp.where(away == doms - 1, 2 - odd, slot)
        slot = jnp.where(away == 2, 3, slot)
        slot = jnp.where(away == doms - 2, 4, slot)
        return slot * 16 + lax.rem(block, 8)

    def attend(b, s):
        places = [place_of(b, j) + s * 8 for j in range(KMAX)]
        keys = jnp.concatenate([kv[place, :, :128] for place in places], axis=0)
        values = jnp.concatenate([kv[place, :, 128:] for place in places], axis=0)
        values = jnp.concatenate([values, jnp.ones_like(values)], axis=1)
        scores = lax.dot_general(
            query[s * 8 + b], keys, (((1,), (1,)), ((), ())), preferred_element_type=f32
        )
        scores = jnp.where(lane_entry < live[b], scores, -1e30)
        top = jnp.max(scores, axis=1, keepdims=True)
        weights = jnp.exp2((scores - top) * scale).astype(bf16)
        mixed = jnp.dot(weights, values, preferred_element_type=f32)
        return (mixed[:, :128] / mixed[:, 128:]).astype(bf16)

    def attend_pair(owner, s):
        return jnp.concatenate([attend(2 * owner + r, s) for r in range(2)], axis=0)

    def h_copy(k, s, src_tp=t):
        owner = lax.rem(t + 1 + k, 4)
        return remote(
            outgoing.at[3 * s + k], heads.at[src_tp, pl.ds(s * 256, 256)], h_s.at[3 * s + k],
            h_r.at[3 * s + k], d, owner,
        )

    def attend_away(s, low, high):
        def one(k, carry):
            outgoing[3 * s + k] = attend_pair(lax.rem(t + 1 + k, 4), s)
            h_copy(k, s).start()
            return carry

        lax.fori_loop(low, high, one, 0)

    def attend_here(s):
        heads[t, s * 256 : (s + 1) * 256] = attend_pair(t, s)

    def spread(ready):
        for w in ready:
            wy_copy(w, across).wait_recv()
            wx_copy(w).start()
            w0_copy(w).start()

    for j in range(3):
        pull(0, j)
        pull_near(0, j)
        if j == 1:
            lax.fori_loop(0, 4, project_own, 0)
    pull_diagonal(0, 0)
    pull_diagonal(0, 1)
    take_direct(0)
    pass_on(0)
    pull(1, 0)
    pull_near(1, 0)
    take_rest(0)
    attend_away(0, 0, 1)
    pull(1, 1)
    pull_near(1, 1)
    attend_away(0, 1, 2)
    pull_diagonal(1, 0)
    attend_away(0, 2, 3)
    pull(1, 2)
    pull_near(1, 2)
    pull_diagonal(1, 1)
    wy_copy(2).start()
    spread((0, 1))
    attend_here(0)
    take_direct(1)
    pass_on(1)
    take_rest(1)
    attend_away(1, 0, 3)
    for w in range(2):
        wx_copy(w, 1 - odd).wait_recv()
        w1_copy(w).start()
    wy_copy(2, across).wait_recv()
    w0_copy(2).start()
    attend_here(1)
    for k in range(3):
        wa_copy(k, sib).wait_recv()
        w0_copy(k, corner).wait_recv()
    for k in range(2):
        w1_copy(k, corner).wait_recv()

    def o_copy(k, s, owner=t):
        peer = lax.rem(t + 1 + k, 4)
        return remote(
            cols.at[peer, pl.ds(s * 256, 256)],
            out.at[s, pl.ds(pl.multiple_of(owner * 256, 256), 256)],
            o_s.at[k, s], o_r.at[k, s], d, peer,
        )

    def finish(s):
        for k in range(3):
            h_copy(k, s, lax.rem(t + 3 - k, 4)).wait_recv()
        rows = slice(s * 256, (s + 1) * 256)
        attn = jnp.zeros((256, 512), f32)
        for h in range(HEADS):
            attn += (
                jnp.dot(heads[h, rows], wout_all[h], preferred_element_type=f32)
                .astype(bf16)
                .astype(f32)
            )
        after = state[pl.ds(8 * s + 2 * t, 2)].reshape(256, 512).astype(f32) + attn
        normed2[...] = layer_norm(after, gain[1, s : s + 1], shift[1, s : s + 1]).astype(bf16)

        def hidden_group(g, total):
            pre = jnp.dot(normed2[...], wup_all[g], preferred_element_type=f32)
            hidden = (0.5 * pre * (1.0 + jnp.tanh(0.5 * pre))).astype(bf16)
            term = jnp.dot(hidden, wdown_all[g], preferred_element_type=f32)
            return total + term.astype(bf16).astype(f32)

        total = lax.fori_loop(0, 4, hidden_group, after, unroll=True)
        for j in range(4):
            cols[j, rows] = total[:, j * 128 : (j + 1) * 128].astype(bf16)
        for k in range(3):
            o_copy(k, s).start()
        out[s, pl.ds(pl.multiple_of(t * 256, 256), 256)] = cols[t, rows]

    for s in range(2):
        finish(s)

    for s in range(2):
        for j in range(3):
            for f in (1, 2):
                z_copy(f, s, j).wait_send()
            n_copy(s, j).wait_send()
            for f in (1, 2, 3):
                a_copy(f, s, j).wait_send()
        for j in range(2):
            x_copy(s, j).wait_send()
            a_copy(0, s, j).wait_send()
        for f, j in crossed:
            y_copy(f, s, j).wait_send()
            b_copy(f, s, j).wait_send()
    for k in range(3):
        for copy in (wy_copy, wa_copy, w0_copy) + ((wx_copy, w1_copy) if k < 2 else ()):
            copy(k).wait_send()
        for s in range(2):
            h_copy(k, s).wait_send()
    for s in range(2):
        for k in range(3):
            o_copy(k, s, lax.rem(t + 3 - k, 4)).wait_recv()
            o_copy(k, s).wait_send()


def local(
    state, norm_gain, norm_shift, qkv_weight, out_weight, up_weight, down_weight, neighbours, counts
):
    samples, row_count, feat = state.shape
    per_dev = row_count // NODE_BLK
    bf16 = jnp.bfloat16
    dma = pltpu.SemaphoreType.DMA
    smem = pl.BlockSpec(memory_space=pltpu.SMEM)
    vmem = pl.BlockSpec(memory_space=pltpu.VMEM)
    anywhere = pl.BlockSpec(memory_space=pl.ANY)
    pairs = [dma((2,)), dma((4,))]
    for shape in [(2, 6), (4, 4), (4, 6), (4, 4), (4,), (6,)] + [(3,)] * 5 + [(6,), (3, 2)]:
        pairs += [dma(shape), dma(shape)]
    return pl.pallas_call(
        layer_kernel,
        out_shape=jax.ShapeDtypeStruct((samples, row_count, 128), bf16),
        in_specs=[smem, smem, vmem, vmem] + [anywhere] * 5,
        out_specs=vmem,
        scratch_shapes=[
            pltpu.VMEM((16, 128, 512), bf16),
            pltpu.VMEM((3, 512, 128), bf16),
            pltpu.VMEM((512, 384), bf16),
            pltpu.VMEM((80, 128, 512), bf16),
            pltpu.VMEM((80, 128, 256), bf16),
            pltpu.VMEM((16, 128, 128), bf16),
            pltpu.VMEM((4, 512, 128), bf16),
            pltpu.VMEM((6, 256, 128), bf16),
            pltpu.VMEM((4, 128, 512), bf16),
            pltpu.VMEM((4, 512, 512), bf16),
            pltpu.VMEM((4, 512, 512), bf16),
            pltpu.VMEM((256, 512), bf16),
            pltpu.VMEM((4, 512, 128), bf16),
        ]
        + pairs,
        compiler_params=pltpu.CompilerParams(
            collective_id=0, has_side_effects=True, vmem_limit_bytes=62 * 2**20
        ),
    )(
        neighbours,
        counts,
        norm_gain,
        norm_shift,
        state.reshape(samples * per_dev, NODE_BLK, feat),
        jnp.transpose(qkv_weight, (1, 0, 2)),
        out_weight,
        up_weight,
        down_weight,
    )


def solution(mesh):
    placed = (
        P(None, "dom", None),
        P(),
        P(),
        P(None, None, "tp"),
        P("tp", None),
        P(None, "tp"),
        P("tp", None),
        P("dom", None),
        P("dom"),
    )
    return jax.shard_map(
        local, mesh=mesh, in_specs=placed, out_specs=P(None, "dom", "tp"), check_vma=False
    )
```

```python
import math

import jax
import jax.numpy as jnp
from jax import lax
from jax.experimental import pallas as pl
from jax.experimental.pallas import tpu as pltpu
from jax.sharding import PartitionSpec as P

HEADS = 4
NODE_BLK = 128
KMAX = 8


def layer_norm(values, gain_row, shift_row):
    row_mean = jnp.mean(values, axis=-1, keepdims=True)
    centred = values - row_mean
    spread = jnp.mean(centred * centred, axis=-1, keepdims=True)
    return centred * lax.rsqrt(spread + 1e-05) * gain_row + shift_row


def layer_kernel(
    neigh, live, gain, shift, state_in, wqkv_in, wout_in, wup_in, wdown_in, out,
    state, wqkv_raw, wqkv, nrm, kv, query, heads, outgoing, wout_all, wup_all, wdown_all, normed2,
    cols, c_state, c_w,
    z_s, z_r, y_s, y_r, a_s, a_r, b_s, b_r, x_s, x_r, n_s, n_r, m_s, m_r,
    wy_s, wy_r, wa_s, wa_r, wx_s, wx_r, w0_s, w0_r, w1_s, w1_r, h_s, h_r, o_s, o_r,
):
    d = lax.axis_index("dom")
    t = lax.axis_index("tp")
    doms = lax.axis_size("dom")
    odd = lax.rem(d, 2)
    near = d + 1 - 2 * odd
    plus = lax.rem(d + 2, doms)
    minus = lax.rem(d + doms - 2, doms)
    core = lax.rem(t, 2)
    sib = t + 1 - 2 * core
    across = lax.rem(t + 2, 4)
    corner = lax.rem(sib + 2, 4)
    f32 = jnp.float32
    bf16 = jnp.bfloat16

    def remote(src, dst, send, recv, dd, tt):
        return pltpu.make_async_remote_copy(
            src_ref=src, dst_ref=dst, send_sem=send, recv_sem=recv, device_id=(dd, tt),
            device_id_type=pl.DeviceIdType.MESH,
        )

    barrier = pltpu.get_barrier_semaphore()
    for partner in [(near, t), (plus, t), (minus, t), (d, sib), (d, across), (d, corner)]:
        pl.semaphore_signal(
            barrier, inc=1, device_id=partner, device_id_type=pl.DeviceIdType.MESH
        )

    def state_copy(s):
        rows = pl.ds(8 * s, 8)
        return pltpu.make_async_copy(state_in.at[rows], state.at[rows], c_state.at[s])

    shards = ((wout_in, wout_all), (wup_in, wup_all), (wdown_in, wdown_all))
    own_copies = [pltpu.make_async_copy(wqkv_in, wqkv_raw, c_w.at[3])] + [
        pltpu.make_async_copy(shard, full.at[t], c_w.at[k])
        for k, (shard, full) in enumerate(shards)
    ]
    for s in range(2):
        state_copy(s).start()
    for copy in own_copies:
        copy.start()

    def norm_units(s, first, count, around=8):
        def norm_one(i, inner):
            u = 8 * s + lax.rem(first + i, around)
            nrm[u] = layer_norm(
                state[u].astype(f32), gain[0, s : s + 1], shift[0, s : s + 1]
            ).astype(bf16)
            return inner

        lax.fori_loop(0, count, norm_one, 0)

    def chunk(slot, s, owner, j):
        u = slot * 16 + 8 * s
        if j == 0:
            return nrm.at[pl.ds(u + 2 * owner, 2)]
        return nrm.at[pl.ds(u + 2 * lax.rem(owner + 2, 4) + 1, 1)]

    def y_chunk(f, s, owner):
        u = (2 + f) * 16 + 8 * s + 2 * owner
        return nrm.at[pl.ds(u, 2 if f == 0 else 1)]

    def z_copy(f, s, j):
        return remote(
            chunk(0, s, t, j), chunk(2 + f, s, t, j), z_s.at[f - 1, 2 * s + j],
            z_r.at[f - 1, 2 * s + j], (minus, plus)[f - 1], t,
        )

    def x_copy(s):
        return remote(
            chunk(3 + odd, s, t, 0), chunk(2, s, t, 0), x_s.at[s], x_r.at[s], near, t
        )

    def y_copy(f, s, owner=t):
        ref = y_chunk(f, s, owner)
        return remote(ref, ref, y_s.at[f, s], y_r.at[f, s], d, across)

    def a_copy(f, s, j, owner=t):
        ref = chunk(2 + f, s, owner, j)
        k = 2 * s + j
        return remote(ref, ref, a_s.at[f, k], a_r.at[f, k], d, sib)

    def b_copy(f, s, owner=across):
        ref = y_chunk(f, s, owner)
        return remote(ref, ref, b_s.at[f, s], b_r.at[f, s], d, sib)

    def n_copy(i):
        u = 8 * (i // 2) + 4 * core + 2 * (i % 2)
        return remote(
            nrm.at[pl.ds(u, 2)], nrm.at[pl.ds(16 + u, 2)], n_s.at[i], n_r.at[i], near, t
        )

    def m_copy(i, side=core):
        u = 16 + 8 * (i // 2) + 4 * side + 2 * (i % 2)
        return remote(nrm.at[pl.ds(u, 2)], nrm.at[pl.ds(u, 2)], m_s.at[i], m_r.at[i], d, sib)

    def part(k, owner, half):
        if k == 2:
            return wdown_all.at[owner]
        rows = shards[k][0].shape[0] // 2
        return shards[k][1].at[owner, pl.ds(pl.multiple_of(half * rows, 64), rows)]

    def wa_copy(k, owner=t):
        full = shards[k][1]
        return remote(full.at[owner], full.at[owner], wa_s.at[k], wa_r.at[k], d, sib)

    def wy_copy(k, owner=t):
        ref = part(k, owner, odd)
        return remote(ref, ref, wy_s.at[k], wy_r.at[k], d, across)

    def wx_copy(k, half=odd):
        ref = part(k, across, half)
        return remote(ref, ref, wx_s.at[k], wx_r.at[k], near, t)

    def w0_copy(k, owner=across):
        ref = part(k, owner, odd)
        return remote(ref, ref, w0_s.at[k], w0_r.at[k], d, sib)

    def w1_copy(k, owner=across):
        ref = part(k, owner, 1 - odd)
        return remote(ref, ref, w1_s.at[k], w1_r.at[k], d, sib)

    state_copy(0).wait()
    norm_units(0, 2 * t, 2)
    pl.semaphore_wait(barrier, 6)
    for f in (1, 2):
        z_copy(f, 0, 0).start()
    norm_units(0, 2 * t + 2, 6)
    for f in (1, 2):
        z_copy(f, 0, 1).start()
    n_copy(0).start()
    n_copy(1).start()
    for copy in own_copies:
        copy.wait()
    for k in range(2):
        wy_copy(k).start()
    state_copy(1).wait()
    norm_units(1, 0, 8)
    for k in range(3):
        wa_copy(k).start()
    for c in range(3):
        wqkv[:, c * 128 : (c + 1) * 128] = wqkv_raw[c]

    def project_own(k, carry):
        rows = pl.ds(4 * k, 4)
        made = jnp.dot(
            nrm[rows].reshape(512, 512), wqkv[...], preferred_element_type=f32
        ).astype(bf16)
        query[rows] = made[:, :128].reshape(4, 128, 128)
        kv[rows] = made[:, 128:].reshape(4, 128, 256)
        return carry


    def project(slot, s, half):
        rows = pl.ds(slot * 16 + 8 * s + 4 * half, 4)
        kv[rows] = (
            jnp.dot(nrm[rows].reshape(512, 512), wqkv[:, 128:], preferred_element_type=f32)
            .astype(bf16)
            .reshape(4, 128, 256)
        )

    def project_slots(s, half, low, high):
        lax.fori_loop(low, high, lambda slot, c: (project(slot, s, half), c)[1], 0)

    def pull(s, j):
        for f in (1, 2):
            z_copy(f, s, j).wait_recv()
            if s == 0:
                z_copy(f, 1, j).start()
        if j == 0:
            x_copy(s).start()
        for f in (1, 2):
            if j == 0:
                y_copy(f, s).start()
            a_copy(f, s, j).start()

    def pull_diagonal(s):
        x_copy(s).wait_recv()
        y_copy(0, s).start()
        a_copy(0, s, 0).start()

    def pull_near(i):
        n_copy(i).wait_recv()
        m_copy(i).start()

    side = lax.div(t, 2)

    def pass_on(s):
        for f in (1, 2, 0):
            y_copy(f, s, across).wait_recv()
            b_copy(f, s).start()

    def take_direct(s):
        for j in range(2):
            for f in (1, 2):
                a_copy(f, s, j, sib).wait_recv()
        for i in (2 * s, 2 * s + 1):
            m_copy(i, 1 - core).wait_recv()
        project_slots(s, 0, 1, 2)
        project_slots(s, 1, 1, 2)
        project_slots(s, side, 3, 5)

    def take_rest(s):
        a_copy(0, s, 0, sib).wait_recv()
        project(2, s, side)
        for f in (1, 2, 0):
            b_copy(f, s, corner).wait_recv()
        project_slots(s, 1 - side, 2, 5)

    scale = math.log2(math.e) / math.sqrt(128)
    lane_entry = lax.broadcasted_iota(jnp.int32, (1, KMAX * NODE_BLK), 1) // NODE_BLK

    def place_of(b, j):
        block = neigh[b, j]
        away = lax.rem(lax.div(block, 8) - d + doms, doms)
        slot = jnp.where(away == 1, 1 + odd, 0)
        slot = jnp.where(away == doms - 1, 2 - odd, slot)
        slot = jnp.where(away == 2, 3, slot)
        slot = jnp.where(away == doms - 2, 4, slot)
        return slot * 16 + lax.rem(block, 8)

    def attend(b, s):
        places = [place_of(b, j) + s * 8 for j in range(KMAX)]
        keys = jnp.concatenate([kv[place, :, :128] for place in places], axis=0)
        values = jnp.concatenate([kv[place, :, 128:] for place in places], axis=0)
        values = jnp.concatenate([values, jnp.ones_like(values)], axis=1)
        scores = lax.dot_general(
            query[s * 8 + b], keys, (((1,), (1,)), ((), ())), preferred_element_type=f32
        )
        scores = jnp.where(lane_entry < live[b], scores, -1e30)
        top = jnp.max(scores, axis=1, keepdims=True)
        weights = jnp.exp2((scores - top) * scale).astype(bf16)
        mixed = jnp.dot(weights, values, preferred_element_type=f32)
        return (mixed[:, :128] / mixed[:, 128:]).astype(bf16)

    def attend_pair(owner, s):
        return jnp.concatenate([attend(2 * owner + r, s) for r in range(2)], axis=0)

    def h_copy(k, s, src_tp=t):
        owner = lax.rem(t + 1 + k, 4)
        return remote(
            outgoing.at[3 * s + k], heads.at[src_tp, pl.ds(s * 256, 256)], h_s.at[3 * s + k],
            h_r.at[3 * s + k], d, owner,
        )

    def attend_away(s, low, high):
        def one(k, carry):
            outgoing[3 * s + k] = attend_pair(lax.rem(t + 1 + k, 4), s)
            h_copy(k, s).start()
            return carry

        lax.fori_loop(low, high, one, 0)

    def attend_here(s):
        heads[t, s * 256 : (s + 1) * 256] = attend_pair(t, s)

    def spread(ready):
        for w in ready:
            wy_copy(w, across).wait_recv()
            wx_copy(w).start()
            w0_copy(w).start()

    pull(0, 0)
    n_copy(2).start()
    lax.fori_loop(0, 4, project_own, 0)
    pull(0, 1)
    n_copy(3).start()
    pull_diagonal(0)
    pull_near(0)
    pull_near(1)
    take_direct(0)
    pass_on(0)
    take_rest(0)
    attend_away(0, 0, 1)
    pull(1, 0)
    attend_away(0, 1, 2)
    pull(1, 1)
    pull_diagonal(1)
    wy_copy(2).start()
    spread((0, 1))
    attend_away(0, 2, 3)
    pull_near(2)
    pull_near(3)
    attend_here(0)
    take_direct(1)
    pass_on(1)
    take_rest(1)
    attend_away(1, 0, 3)
    for w in range(2):
        wx_copy(w, 1 - odd).wait_recv()
        w1_copy(w).start()
    wy_copy(2, across).wait_recv()
    w0_copy(2).start()
    attend_here(1)
    for k in range(3):
        wa_copy(k, sib).wait_recv()
        w0_copy(k, corner).wait_recv()
    for k in range(2):
        w1_copy(k, corner).wait_recv()

    def o_copy(k, s, owner=t):
        peer = lax.rem(t + 1 + k, 4)
        return remote(
            cols.at[peer, pl.ds(s * 256, 256)],
            out.at[s, pl.ds(pl.multiple_of(owner * 256, 256), 256)],
            o_s.at[k, s], o_r.at[k, s], d, peer,
        )

    def finish(s):
        for k in range(3):
            h_copy(k, s, lax.rem(t + 3 - k, 4)).wait_recv()
        rows = slice(s * 256, (s + 1) * 256)
        attn = jnp.zeros((256, 512), f32)
        for h in range(HEADS):
            attn += (
                jnp.dot(heads[h, rows], wout_all[h], preferred_element_type=f32)
                .astype(bf16)
                .astype(f32)
            )
        after = state[pl.ds(8 * s + 2 * t, 2)].reshape(256, 512).astype(f32) + attn
        normed2[...] = layer_norm(after, gain[1, s : s + 1], shift[1, s : s + 1]).astype(bf16)

        def hidden_group(g, total):
            pre = jnp.dot(normed2[...], wup_all[g], preferred_element_type=f32)
            hidden = (0.5 * pre * (1.0 + jnp.tanh(0.5 * pre))).astype(bf16)
            term = jnp.dot(hidden, wdown_all[g], preferred_element_type=f32)
            return total + term.astype(bf16).astype(f32)

        total = lax.fori_loop(0, 4, hidden_group, after, unroll=True)
        for j in range(4):
            cols[j, rows] = total[:, j * 128 : (j + 1) * 128].astype(bf16)
        for k in range(3):
            o_copy(k, s).start()
        out[s, pl.ds(pl.multiple_of(t * 256, 256), 256)] = cols[t, rows]

    for s in range(2):
        finish(s)

    for s in range(2):
        for j in range(2):
            for f in (1, 2):
                z_copy(f, s, j).wait_send()
                a_copy(f, s, j).wait_send()
        x_copy(s).wait_send()
        a_copy(0, s, 0).wait_send()
        for f in range(3):
            y_copy(f, s).wait_send()
            b_copy(f, s).wait_send()
    for i in range(4):
        n_copy(i).wait_send()
        m_copy(i).wait_send()
    for k in range(3):
        for copy in (wy_copy, wa_copy, w0_copy) + ((wx_copy, w1_copy) if k < 2 else ()):
            copy(k).wait_send()
        for s in range(2):
            h_copy(k, s).wait_send()
    for s in range(2):
        for k in range(3):
            o_copy(k, s, lax.rem(t + 3 - k, 4)).wait_recv()
            o_copy(k, s).wait_send()


def local(
    state, norm_gain, norm_shift, qkv_weight, out_weight, up_weight, down_weight, neighbours, counts
):
    samples, row_count, feat = state.shape
    per_dev = row_count // NODE_BLK
    bf16 = jnp.bfloat16
    dma = pltpu.SemaphoreType.DMA
    smem = pl.BlockSpec(memory_space=pltpu.SMEM)
    vmem = pl.BlockSpec(memory_space=pltpu.VMEM)
    anywhere = pl.BlockSpec(memory_space=pl.ANY)
    pairs = [dma((2,)), dma((4,))]
    for shape in [(2, 4), (3, 2), (3, 4), (3, 2), (2,), (4,), (4,)] + [(3,)] * 5 + [(6,), (3, 2)]:
        pairs += [dma(shape), dma(shape)]
    return pl.pallas_call(
        layer_kernel,
        out_shape=jax.ShapeDtypeStruct((samples, row_count, 128), bf16),
        in_specs=[smem, smem, vmem, vmem] + [anywhere] * 5,
        out_specs=vmem,
        scratch_shapes=[
            pltpu.VMEM((16, 128, 512), bf16),
            pltpu.VMEM((3, 512, 128), bf16),
            pltpu.VMEM((512, 384), bf16),
            pltpu.VMEM((80, 128, 512), bf16),
            pltpu.VMEM((80, 128, 256), bf16),
            pltpu.VMEM((16, 128, 128), bf16),
            pltpu.VMEM((4, 512, 128), bf16),
            pltpu.VMEM((6, 256, 128), bf16),
            pltpu.VMEM((4, 128, 512), bf16),
            pltpu.VMEM((4, 512, 512), bf16),
            pltpu.VMEM((4, 512, 512), bf16),
            pltpu.VMEM((256, 512), bf16),
            pltpu.VMEM((4, 512, 128), bf16),
        ]
        + pairs,
        compiler_params=pltpu.CompilerParams(
            collective_id=0, has_side_effects=True, vmem_limit_bytes=62 * 2**20
        ),
    )(
        neighbours,
        counts,
        norm_gain,
        norm_shift,
        state.reshape(samples * per_dev, NODE_BLK, feat),
        jnp.transpose(qkv_weight, (1, 0, 2)),
        out_weight,
        up_weight,
        down_weight,
    )


def solution(mesh):
    placed = (
        P(None, "dom", None),
        P(),
        P(),
        P(None, None, "tp"),
        P("tp", None),
        P(None, "tp"),
        P("tp", None),
        P("dom", None),
        P("dom"),
    )
    return jax.shard_map(
        local, mesh=mesh, in_specs=placed, out_specs=P(None, "dom", "tp"), check_vma=False
    )
```

```python
import math

import jax
import jax.numpy as jnp
from jax import lax
from jax.experimental import pallas as pl
from jax.experimental.pallas import tpu as pltpu
from jax.sharding import PartitionSpec as P

HEADS = 4
NODE_BLK = 128
KMAX = 8


def layer_norm(values, gain_row, shift_row):
    row_mean = jnp.mean(values, axis=-1, keepdims=True)
    centred = values - row_mean
    spread = jnp.mean(centred * centred, axis=-1, keepdims=True)
    return centred * lax.rsqrt(spread + 1e-05) * gain_row + shift_row


def layer_kernel(
    neigh, live, gain, shift, state_in, wqkv_in, wout_in, wup_in, wdown_in, out,
    state, wqkv_raw, wqkv, nrm, kv, query, heads, outgoing, wout_all, wup_all, wdown_all, normed2,
    cols, c_state, c_w,
    z_s, z_r, y_s, y_r, a_s, a_r, b_s, b_r, x_s, x_r, n_s, n_r, m_s, m_r,
    wy_s, wy_r, wa_s, wa_r, wx_s, wx_r, w0_s, w0_r, w1_s, w1_r, h_s, h_r, o_s, o_r,
):
    d = lax.axis_index("dom")
    t = lax.axis_index("tp")
    doms = lax.axis_size("dom")
    odd = lax.rem(d, 2)
    near = d + 1 - 2 * odd
    plus = lax.rem(d + 2, doms)
    minus = lax.rem(d + doms - 2, doms)
    core = lax.rem(t, 2)
    sib = t + 1 - 2 * core
    across = lax.rem(t + 2, 4)
    corner = lax.rem(sib + 2, 4)
    f32 = jnp.float32
    bf16 = jnp.bfloat16

    def remote(src, dst, send, recv, dd, tt):
        return pltpu.make_async_remote_copy(
            src_ref=src, dst_ref=dst, send_sem=send, recv_sem=recv, device_id=(dd, tt),
            device_id_type=pl.DeviceIdType.MESH,
        )

    barrier = pltpu.get_barrier_semaphore()
    for partner in [(near, t), (plus, t), (minus, t), (d, sib), (d, across), (d, corner)]:
        pl.semaphore_signal(
            barrier, inc=1, device_id=partner, device_id_type=pl.DeviceIdType.MESH
        )

    def state_copy(s):
        rows = pl.ds(8 * s, 8)
        return pltpu.make_async_copy(state_in.at[rows], state.at[rows], c_state.at[s])

    shards = ((wout_in, wout_all), (wup_in, wup_all), (wdown_in, wdown_all))
    own_copies = [pltpu.make_async_copy(wqkv_in, wqkv_raw, c_w.at[3])] + [
        pltpu.make_async_copy(shard, full.at[t], c_w.at[k])
        for k, (shard, full) in enumerate(shards)
    ]
    for s in range(2):
        state_copy(s).start()
    for copy in own_copies:
        copy.start()

    def norm_units(s, first, count, around=8):
        def norm_one(i, inner):
            u = 8 * s + lax.rem(first + i, around)
            nrm[u] = layer_norm(
                state[u].astype(f32), gain[0, s : s + 1], shift[0, s : s + 1]
            ).astype(bf16)
            return inner

        lax.fori_loop(0, count, norm_one, 0)

    def unit(rank, j):
        side = lax.div(rank, 2)
        shared = 4 + 2 * lax.rem(rank, 2)
        return (rank, shared + side, shared + 1 - side)[j]

    def z_copy(f, s, j):
        u = 8 * s + unit(t, j)
        return remote(
            nrm.at[u], nrm.at[(2 + f) * 16 + u], z_s.at[f - 1, 3 * s + j],
            z_r.at[f - 1, 3 * s + j], (minus, plus)[f - 1], t,
        )

    def x_copy(s, j):
        u = 8 * s + unit(t, j)
        k = 2 * s + j
        return remote(
            nrm.at[(3 + odd) * 16 + u], nrm.at[2 * 16 + u], x_s.at[k], x_r.at[k], near, t
        )

    def y_copy(f, s, j, owner=t):
        u = (2 + f) * 16 + 8 * s + unit(owner, j)
        k = 2 * s + j
        return remote(nrm.at[u], nrm.at[u], y_s.at[f, k], y_r.at[f, k], d, across)

    def a_copy(f, s, j, owner=t):
        u = (2 + f) * 16 + 8 * s + unit(owner, j)
        k = 3 * s + j
        return remote(nrm.at[u], nrm.at[u], a_s.at[f, k], a_r.at[f, k], d, sib)

    def b_copy(f, s, j, owner=across):
        u = (2 + f) * 16 + 8 * s + unit(owner, j)
        k = 2 * s + j
        return remote(nrm.at[u], nrm.at[u], b_s.at[f, k], b_r.at[f, k], d, sib)

    def n_copy(i):
        u = 8 * (i // 2) + 4 * core + 2 * (i % 2)
        return remote(
            nrm.at[pl.ds(u, 2)], nrm.at[pl.ds(16 + u, 2)], n_s.at[i], n_r.at[i], near, t
        )

    def m_copy(i, side=core):
        u = 16 + 8 * (i // 2) + 4 * side + 2 * (i % 2)
        return remote(nrm.at[pl.ds(u, 2)], nrm.at[pl.ds(u, 2)], m_s.at[i], m_r.at[i], d, sib)

    def part(k, owner, half):
        if k == 2:
            return wdown_all.at[owner]
        rows = shards[k][0].shape[0] // 2
        return shards[k][1].at[owner, pl.ds(pl.multiple_of(half * rows, 64), rows)]

    def wa_copy(k, owner=t):
        full = shards[k][1]
        return remote(full.at[owner], full.at[owner], wa_s.at[k], wa_r.at[k], d, sib)

    def wy_copy(k, owner=t):
        ref = part(k, owner, odd)
        return remote(ref, ref, wy_s.at[k], wy_r.at[k], d, across)

    def wx_copy(k, half=odd):
        ref = part(k, across, half)
        return remote(ref, ref, wx_s.at[k], wx_r.at[k], near, t)

    def w0_copy(k, owner=across):
        ref = part(k, owner, odd)
        return remote(ref, ref, w0_s.at[k], w0_r.at[k], d, sib)

    def w1_copy(k, owner=across):
        ref = part(k, owner, 1 - odd)
        return remote(ref, ref, w1_s.at[k], w1_r.at[k], d, sib)

    state_copy(0).wait()
    norm_units(0, t, 1)
    norm_units(0, 4 + 2 * core, 2)
    pl.semaphore_wait(barrier, 6)
    for j in range(3):
        for f in (1, 2):
            z_copy(f, 0, j).start()
    norm_units(0, t + 1, 3, 4)
    norm_units(0, 6 - 2 * core, 2)
    n_copy(0).start()
    for copy in own_copies:
        copy.wait()
    for k in range(2):
        wy_copy(k).start()
    state_copy(1).wait()
    norm_units(1, 0, 8)
    for k in range(3):
        wa_copy(k).start()
    for c in range(3):
        wqkv[:, c * 128 : (c + 1) * 128] = wqkv_raw[c]

    def project_own(k, carry):
        rows = pl.ds(4 * k, 4)
        made = jnp.dot(
            nrm[rows].reshape(512, 512), wqkv[...], preferred_element_type=f32
        ).astype(bf16)
        query[rows] = made[:, :128].reshape(4, 128, 128)
        kv[rows] = made[:, 128:].reshape(4, 128, 256)
        return carry


    def project(slot, s, half):
        rows = pl.ds(slot * 16 + 8 * s + 4 * half, 4)
        kv[rows] = (
            jnp.dot(nrm[rows].reshape(512, 512), wqkv[:, 128:], preferred_element_type=f32)
            .astype(bf16)
            .reshape(4, 128, 256)
        )

    def project_slots(s, half, low, high):
        lax.fori_loop(low, high, lambda slot, c: (project(slot, s, half), c)[1], 0)

    def pull(s, j):
        for f in (1, 2):
            z_copy(f, s, j).wait_recv()
            if s == 0:
                z_copy(f, 1, j).start()
        if j < 2:
            x_copy(s, j).start()
        for f in (1, 2):
            if j == 0:
                y_copy(f, s, 0).start()
            a_copy(f, s, j).start()

    def pull_diagonal(s, j):
        x_copy(s, j).wait_recv()
        y_copy(0, s, j).start()
        a_copy(0, s, j).start()

    def pull_near(i):
        n_copy(i).wait_recv()
        m_copy(i).start()

    crossed = ((1, 0), (2, 0), (0, 0), (0, 1))

    def pass_on(s):
        for f, j in crossed:
            y_copy(f, s, j, across).wait_recv()
            b_copy(f, s, j).start()

    def take_direct(s):
        for j in range(3):
            for f in (1, 2):
                a_copy(f, s, j, sib).wait_recv()
        for i in (2 * s, 2 * s + 1):
            m_copy(i, 1 - core).wait_recv()
        project_slots(s, 0, 1, 2)
        project_slots(s, 1, 1, 2)
        project_slots(s, 1, 3, 5)

    def take_rest(s):
        for j in range(2):
            a_copy(0, s, j, sib).wait_recv()
        for f, j in crossed:
            b_copy(f, s, j, corner).wait_recv()
        project_slots(s, 0, 2, 5)
        project_slots(s, 1, 2, 3)

    scale = math.log2(math.e) / math.sqrt(128)
    lane_entry = lax.broadcasted_iota(jnp.int32, (1, KMAX * NODE_BLK), 1) // NODE_BLK

    def place_of(b, j):
        block = neigh[b, j]
        away = lax.rem(lax.div(block, 8) - d + doms, doms)
        slot = jnp.where(away == 1, 1 + odd, 0)
        slot = jnp.where(away == doms - 1, 2 - odd, slot)
        slot = jnp.where(away == 2, 3, slot)
        slot = jnp.where(away == doms - 2, 4, slot)
        return slot * 16 + lax.rem(block, 8)

    def attend(b, s):
        places = [place_of(b, j) + s * 8 for j in range(KMAX)]
        keys = jnp.concatenate([kv[place, :, :128] for place in places], axis=0)
        values = jnp.concatenate([kv[place, :, 128:] for place in places], axis=0)
        values = jnp.concatenate([values, jnp.ones_like(values)], axis=1)
        scores = lax.dot_general(
            query[s * 8 + b], keys, (((1,), (1,)), ((), ())), preferred_element_type=f32
        )
        scores = jnp.where(lane_entry < live[b], scores, -1e30)
        top = jnp.max(scores, axis=1, keepdims=True)
        weights = jnp.exp2((scores - top) * scale).astype(bf16)
        mixed = jnp.dot(weights, values, preferred_element_type=f32)
        return (mixed[:, :128] / mixed[:, 128:]).astype(bf16)

    def attend_pair(owner, s):
        return jnp.concatenate([attend(2 * owner + r, s) for r in range(2)], axis=0)

    def h_copy(k, s, src_tp=t):
        owner = lax.rem(t + 1 + k, 4)
        return remote(
            outgoing.at[3 * s + k], heads.at[src_tp, pl.ds(s * 256, 256)], h_s.at[3 * s + k],
            h_r.at[3 * s + k], d, owner,
        )

    def attend_away(s, low, high):
        def one(k, carry):
            outgoing[3 * s + k] = attend_pair(lax.rem(t + 1 + k, 4), s)
            h_copy(k, s).start()
            return carry

        lax.fori_loop(low, high, one, 0)

    def attend_here(s):
        heads[t, s * 256 : (s + 1) * 256] = attend_pair(t, s)

    def spread(ready):
        for w in ready:
            wy_copy(w, across).wait_recv()
            wx_copy(w).start()
            w0_copy(w).start()

    for j in range(3):
        pull(0, j)
        if j == 1:
            n_copy(1).start()
            lax.fori_loop(0, 4, project_own, 0)
    pull_diagonal(0, 0)
    pull_diagonal(0, 1)
    pull_near(0)
    pull_near(1)
    take_direct(0)
    pass_on(0)
    pull(1, 0)
    n_copy(2).start()
    take_rest(0)
    attend_away(0, 0, 1)
    pull(1, 1)
    n_copy(3).start()
    attend_away(0, 1, 2)
    pull_diagonal(1, 0)
    attend_away(0, 2, 3)
    pull(1, 2)
    pull_diagonal(1, 1)
    wy_copy(2).start()
    spread((0, 1))
    pull_near(2)
    pull_near(3)
    attend_here(0)
    take_direct(1)
    pass_on(1)
    take_rest(1)
    attend_away(1, 0, 3)
    for w in range(2):
        wx_copy(w, 1 - odd).wait_recv()
        w1_copy(w).start()
    wy_copy(2, across).wait_recv()
    w0_copy(2).start()
    attend_here(1)
    for k in range(3):
        wa_copy(k, sib).wait_recv()
        w0_copy(k, corner).wait_recv()
    for k in range(2):
        w1_copy(k, corner).wait_recv()

    def o_copy(k, s, owner=t):
        peer = lax.rem(t + 1 + k, 4)
        return remote(
            cols.at[peer, pl.ds(s * 256, 256)],
            out.at[s, pl.ds(pl.multiple_of(owner * 256, 256), 256)],
            o_s.at[k, s], o_r.at[k, s], d, peer,
        )

    def finish(s):
        for k in range(3):
            h_copy(k, s, lax.rem(t + 3 - k, 4)).wait_recv()
        rows = slice(s * 256, (s + 1) * 256)
        attn = jnp.zeros((256, 512), f32)
        for h in range(HEADS):
            attn += (
                jnp.dot(heads[h, rows], wout_all[h], preferred_element_type=f32)
                .astype(bf16)
                .astype(f32)
            )
        after = state[pl.ds(8 * s + 2 * t, 2)].reshape(256, 512).astype(f32) + attn
        normed2[...] = layer_norm(after, gain[1, s : s + 1], shift[1, s : s + 1]).astype(bf16)

        def hidden_group(g, total):
            pre = jnp.dot(normed2[...], wup_all[g], preferred_element_type=f32)
            hidden = (0.5 * pre * (1.0 + jnp.tanh(0.5 * pre))).astype(bf16)
            term = jnp.dot(hidden, wdown_all[g], preferred_element_type=f32)
            return total + term.astype(bf16).astype(f32)

        total = lax.fori_loop(0, 4, hidden_group, after, unroll=True)
        for j in range(4):
            cols[j, rows] = total[:, j * 128 : (j + 1) * 128].astype(bf16)
        for k in range(3):
            o_copy(k, s).start()
        out[s, pl.ds(pl.multiple_of(t * 256, 256), 256)] = cols[t, rows]

    for s in range(2):
        finish(s)

    for s in range(2):
        for j in range(3):
            for f in (1, 2):
                z_copy(f, s, j).wait_send()
                a_copy(f, s, j).wait_send()
        for j in range(2):
            x_copy(s, j).wait_send()
            a_copy(0, s, j).wait_send()
        for f, j in crossed:
            y_copy(f, s, j).wait_send()
            b_copy(f, s, j).wait_send()
    for i in range(4):
        n_copy(i).wait_send()
        m_copy(i).wait_send()
    for k in range(3):
        for copy in (wy_copy, wa_copy, w0_copy) + ((wx_copy, w1_copy) if k < 2 else ()):
            copy(k).wait_send()
        for s in range(2):
            h_copy(k, s).wait_send()
    for s in range(2):
        for k in range(3):
            o_copy(k, s, lax.rem(t + 3 - k, 4)).wait_recv()
            o_copy(k, s).wait_send()


def local(
    state, norm_gain, norm_shift, qkv_weight, out_weight, up_weight, down_weight, neighbours, counts
):
    samples, row_count, feat = state.shape
    per_dev = row_count // NODE_BLK
    bf16 = jnp.bfloat16
    dma = pltpu.SemaphoreType.DMA
    smem = pl.BlockSpec(memory_space=pltpu.SMEM)
    vmem = pl.BlockSpec(memory_space=pltpu.VMEM)
    anywhere = pl.BlockSpec(memory_space=pl.ANY)
    pairs = [dma((2,)), dma((4,))]
    for shape in [(2, 6), (3, 4), (3, 6), (3, 4)] + [(4,)] * 3 + [(3,)] * 5 + [(6,), (3, 2)]:
        pairs += [dma(shape), dma(shape)]
    return pl.pallas_call(
        layer_kernel,
        out_shape=jax.ShapeDtypeStruct((samples, row_count, 128), bf16),
        in_specs=[smem, smem, vmem, vmem] + [anywhere] * 5,
        out_specs=vmem,
        scratch_shapes=[
            pltpu.VMEM((16, 128, 512), bf16),
            pltpu.VMEM((3, 512, 128), bf16),
            pltpu.VMEM((512, 384), bf16),
            pltpu.VMEM((80, 128, 512), bf16),
            pltpu.VMEM((80, 128, 256), bf16),
            pltpu.VMEM((16, 128, 128), bf16),
            pltpu.VMEM((4, 512, 128), bf16),
            pltpu.VMEM((6, 256, 128), bf16),
            pltpu.VMEM((4, 128, 512), bf16),
            pltpu.VMEM((4, 512, 512), bf16),
            pltpu.VMEM((4, 512, 512), bf16),
            pltpu.VMEM((256, 512), bf16),
            pltpu.VMEM((4, 512, 128), bf16),
        ]
        + pairs,
        compiler_params=pltpu.CompilerParams(
            collective_id=0, has_side_effects=True, vmem_limit_bytes=62 * 2**20
        ),
    )(
        neighbours,
        counts,
        norm_gain,
        norm_shift,
        state.reshape(samples * per_dev, NODE_BLK, feat),
        jnp.transpose(qkv_weight, (1, 0, 2)),
        out_weight,
        up_weight,
        down_weight,
    )


def solution(mesh):
    placed = (
        P(None, "dom", None),
        P(),
        P(),
        P(None, None, "tp"),
        P("tp", None),
        P(None, "tp"),
        P("tp", None),
        P("dom", None),
        P("dom"),
    )
    return jax.shard_map(
        local, mesh=mesh, in_specs=placed, out_specs=P(None, "dom", "tp"), check_vma=False
    )
```
